128 devices in a mesh: outer: 16 (over y, x_hi, core), inner: 8 (over z, x_lo).
Axes of the slice: x: 4 (x_hi: 2, x_lo: 2; x = x_hi * 2 + x_lo), y: 4, z: 4, core: 2. Of those that a mesh axis runs over, the one named last changes fastest.
Arguments:
- queries: bfloat16 [14336, 4096], P(('outer', 'inner')), may hold values from -130 to 130
- keys: bfloat16 [14336, 512], P(('outer', 'inner')), may hold values from -5.1 to 5.1
- values: bfloat16 [14336, 512], P(('outer', 'inner')), may hold values from -6 to 6
- positions: int32 [14336], P(('outer', 'inner')), may hold values from 0 to 14335, as said below
Outputs:
- attended: bfloat16 [14336, 4096], P(('outer', 'inner'))
The draws below stay inside these ranges and needn't reach their ends.
Inputs may be any that keep to these rules, and one draw needn't show every extreme that they name: positions is a permutation of 0 to 14335 made of runs: rows r * 56 to (r + 1) * 56 - 1 hold 56 consecutive positions starting at a multiple of 56, in increasing order.
All inputs are finite; a program needn't handle non-finite values.
Results may differ from the reference program's by a relative error of at most 0.0065.
Values may be sent and summed in bfloat16 or wider, within the bound.
A program may use at most 128 MiB of HBM per device.

```python
import math
import jax
import jax.numpy as jnp
from jax import lax

HEADS = 32
KV_HEADS = 4
HEAD_DIM = 128
GROUP = 8
SPAN = 56
SEQ = 14336


def common_keys(key):
    return jax.random.truncated_normal(jax.random.fold_in(key, 11), -5.0, 5.0, (SEQ, KV_HEADS, HEAD_DIM), jnp.float32)


def draw_keys(key, part):
    base = common_keys(key)
    return base.reshape(SEQ, KV_HEADS * HEAD_DIM).astype(jnp.bfloat16)


def draw_queries(key, part):
    key = jax.random.fold_in(key, 5)
    result = jax.random.truncated_normal(key, -5.0, 5.0, (SEQ, HEADS, HEAD_DIM), jnp.float32) * 2.5
    return result.reshape(SEQ, HEADS * HEAD_DIM).astype(jnp.bfloat16)


def draw_positions(key, part):
    key = jax.random.fold_in(key, 7)
    order = jax.random.permutation(key, SEQ // SPAN).astype(jnp.int32)
    row_ids = jnp.arange(SEQ, dtype=jnp.int32)
    return (order[row_ids // SPAN] * SPAN + row_ids % SPAN).astype(jnp.int32)


def steps_of(stream_key, shape, cuts, least, high):
    factor_of, own = 1.0, jax.random.fold_in(stream_key, 6)
    for position, shards_of in cuts:
        draws = jnp.exp(jax.random.uniform(jax.random.fold_in(own, position), (shards_of,), jnp.float32, least / len(cuts), high / len(cuts)))
        factor_of = factor_of * jnp.repeat(draws, shape[position] // shards_of).reshape([-1 if axis == position else 1 for axis in range(len(shape))])
    return factor_of


def gaussian(own_key, shape, deviation, bound, cuts=(), kind=jnp.bfloat16):
    drawn = deviation * jax.random.normal(own_key, shape, jnp.float32)
    if cuts:
        drawn = drawn * steps_of(own_key, shape, cuts, -0.22, 0.18)
    return jnp.clip(drawn, -bound, bound).astype(kind)


def setup_inputs(seed: int = 0) -> dict:
    streams_of = jax.random.split(jax.random.key(seed), 5)
    return {
        "queries": draw_queries(jax.random.fold_in(streams_of[4], 71), 0),
        "keys": draw_keys(jax.random.fold_in(streams_of[4], 71), 0),
        "values": gaussian(streams_of[2], (SEQ, KV_HEADS * HEAD_DIM), 1.0, 6.0, ((0, 128),)),
        "positions": draw_positions(jax.random.fold_in(streams_of[4], 71), 0),
    }


def reference(queries, keys, values, positions):
    score_scale = HEAD_DIM ** -0.5
    key_heads = keys.astype(jnp.float32).reshape(SEQ, KV_HEADS, HEAD_DIM)
    value_heads = values.astype(jnp.float32).reshape(SEQ, KV_HEADS, HEAD_DIM)
    block_rows = math.gcd(SEQ, 256)
    query_blocks = queries.reshape(SEQ // block_rows, block_rows, KV_HEADS, GROUP, HEAD_DIM)
    pos_blocks = positions.reshape(SEQ // block_rows, block_rows)

    def one_block(packed):
        query_block, pos_block = packed
        scores = jnp.einsum("qhgd,khd->hgqk", query_block.astype(jnp.float32), key_heads) * score_scale
        visible = positions[None, :] <= pos_block[:, None]
        masked = jnp.where(visible, scores, -1e30)
        top = jnp.max(masked, axis=-1)
        weights = jnp.where(visible, jnp.exp(masked - top[..., None]), 0.0)
        total = jnp.sum(weights, axis=-1)
        rounded = lax.optimization_barrier(weights.astype(jnp.bfloat16))
        summed = jnp.einsum("hgqk,khd->qhgd", rounded.astype(jnp.float32), value_heads)
        result = summed / jnp.transpose(total, (2, 0, 1))[..., None]
        return result.reshape(block_rows, HEADS * HEAD_DIM).astype(jnp.bfloat16)

    outputs = lax.map(one_block, (query_blocks, pos_blocks))
    return outputs.reshape(SEQ, HEADS * HEAD_DIM)
```

```python
import functools
import jax
import jax.numpy as jnp
from jax import lax
from jax.experimental import pallas as pl
from jax.experimental.pallas import tpu as pltpu
from jax.sharding import PartitionSpec as P

HEADS = 32
KV_HEADS = 4
D = 128
SPAN = 56
SEQ = 14336
RUNS = SEQ // SPAN
ROWS = 112
PEERS = 16
MESH = pl.DeviceIdType.MESH
LOG2E = 1.4426950408889634
SCALE = D ** -0.5 * LOG2E
HBM = pl.ANY
KEY_TILE = 1024
CHUNK = 256
TILE_RUNS = 4
HEADS_HERE = 2
TILE_ROWS = TILE_RUNS * SPAN
M = HEADS_HERE * TILE_ROWS
GROUP_RUNS = 2 * PEERS
SAFE = 90.0


def coords():
    outer, inner = lax.axis_index("outer"), lax.axis_index("inner")
    y, xh, core = outer // 4, (outer // 2) % 2, outer % 2
    return xh * 2 + inner % 2, y, inner // 2, core


def at(x, y, z, core):
    return ((y * 4 + (x // 2) * 2 + core), z * 2 + x % 2)


def greet(devices):
    barrier = pltpu.get_barrier_semaphore()
    for device in devices:
        pl.semaphore_signal(barrier, inc=1, device_id=device, device_id_type=MESH)
    pl.semaphore_wait(barrier, len(devices))


def group_peers(x, y, z, core):
    peers = []
    for d in range(1, PEERS):
        zz = (z + d // 4) % 4
        xx = (x // 2) * 2 + (x % 2 + (d // 2) % 2) % 2
        cc = (core + d % 2) % 2
        peers.append((xx, y, zz, cc))
    return peers


def slot_of(x, z, core):
    return z * 4 + (x % 2) * 2 + core


def gather_kernel(q_ref, k_ref, v_ref, qg_ref, kg_ref, vg_ref,
                  q_send, q_recv, z_send, z_recv, l_sem,
                  a_send, a_recv, b_send, b_recv, s_send, s_recv):
    x, y, z, core = coords()
    xr, xl, xo = (x + 1) % 4, (x + 3) % 4, (x + 2) % 4
    yr, yl, yo = (y + 1) % 4, (y + 3) % 4, (y + 2) % 4
    peers = group_peers(x, y, z, core)
    far_x = (x // 2) * 2 + (x + 1) % 2
    other_x = jnp.where(far_x == xr, xl, xr)
    greet([at(*p) for p in peers]
          + [at(other_x, y, z, core), at(x, yr, z, core), at(x, yl, z, core)])

    sent = []

    def send(src, dst, ssem, rsem, to):
        c = pltpu.make_async_remote_copy(
            src_ref=src, dst_ref=dst, send_sem=ssem, recv_sem=rsem,
            device_id=at(*to), device_id_type=MESH)
        c.start()
        sent.append(c)
        return c

    arrays = ((k_ref, kg_ref), (v_ref, vg_ref))
    zc = []
    for d in range(1, 4):
        zz = (z + d) % 4
        for i, (src, dst) in enumerate(arrays):
            zc.append(send(src.at[:, pl.ds(pl.multiple_of(zz * D, D), D)],
                           dst.at[core, y, x, pl.ds(pl.multiple_of(z * ROWS, 16), ROWS), :],
                           z_send.at[i, d], z_recv.at[i, d], (x, y, zz, core)))
    lc = []
    for i, (src, dst) in enumerate(arrays):
        c = pltpu.make_async_copy(src.at[:, pl.ds(pl.multiple_of(z * D, D), D)],
                                  dst.at[core, y, x, pl.ds(pl.multiple_of(z * ROWS, 16), ROWS), :],
                                  l_sem.at[i])
        c.start()
        lc.append(c)
    me = slot_of(x, z, core)
    qc = []
    for d, p in zip(range(1, PEERS), peers):
        t = slot_of(p[0], p[2], p[3])
        qc.append(send(q_ref.at[:, pl.ds(pl.multiple_of(t * 256, 256), 256)],
                       qg_ref.at[me], q_send.at[d], q_recv.at[d], p))
    c = pltpu.make_async_copy(q_ref.at[:, pl.ds(pl.multiple_of(me * 256, 256), 256)],
                              qg_ref.at[me], l_sem.at[2])
    c.start()
    lc.append(c)
    for c in zc:
        c.wait_recv()
    for c in lc:
        c.wait()

    half = 2 * ROWS

    def block(i, bx, by, h=None):
        ref = arrays[i][1]
        if h is None:
            return ref.at[core, by, bx]
        return ref.at[core, by, bx, pl.ds(h * half, half), :]

    sibling = (x, y, z, 1 - core)
    ring = (((xl, y), (xr, y)), ((x, yl), (x, yr)))
    cross = (((x, yl), (x, yr)), ((xl, y), (xr, y)))

    def to(pos):
        return (pos[0], pos[1], z, core)

    def hand(i, n, bx, by):
        ref = block(i, bx, by)
        return send(ref, ref, s_send.at[i, n], s_recv.at[i, n], sibling)

    sib = []

    def first(i):
        ref = block(i, x, y)
        lo, hi = ring[i]
        up = send(ref, ref, a_send.at[i, 0], a_recv.at[i, 0], to(hi))
        dn = send(ref, ref, a_send.at[i, 1], a_recv.at[i, 1], to(lo))
        return up, dn

    def second(i, n, bx, by):
        ref = block(i, bx, by)
        lo, hi = cross[i]
        up = send(ref, ref, b_send.at[i, n, 0], b_recv.at[i, n, 0], to(hi))
        dn = send(ref, ref, b_send.at[i, n, 1], b_recv.at[i, n, 1], to(lo))
        sib.append(hand(i, 4 * n, bx, by))
        return up, dn

    def along(i, bx, by, n):
        if i == 0:
            return ((bx, by), (xl, by), (xr, by), (xo, by))[n]
        return ((bx, by), (bx, yl), (bx, yr), (bx, yo))[n]

    def across(i, bx, by, n):
        if i == 0:
            return ((bx, by), (bx, yl), (bx, yr), (bx, yo))[n]
        return ((bx, by), (xl, by), (xr, by), (xo, by))[n]

    a = [first(0), first(1)]
    b = [[second(0, 0, x, y)], [second(1, 0, x, y)]]
    fwd = [None, None]
    for i in range(2):
        up, dn = a[i]
        lo, hi = ring[i]
        up.wait_recv()
        bx, by = along(i, x, y, 1)
        f1 = send(block(i, bx, by, 0), block(i, bx, by, 0), a_send.at[i, 2], a_recv.at[i, 2], to(hi))
        dn.wait_recv()
        cx, cy = along(i, x, y, 2)
        f2 = send(block(i, cx, cy, 1), block(i, cx, cy, 1), a_send.at[i, 3], a_recv.at[i, 3], to(lo))
        fwd[i] = (f1, f2)
        b[i].append(second(i, 1, bx, by))
        b[i].append(second(i, 2, cx, cy))

    def relay(i, n):
        bx, by = along(i, x, y, n)
        up, dn = b[i][n]
        lo, hi = cross[i]
        up.wait_recv()
        ux, uy = across(i, bx, by, 1)
        f1 = send(block(i, ux, uy, 0), block(i, ux, uy, 0), b_send.at[i, n, 2], b_recv.at[i, n, 2], to(hi))
        sib.append(hand(i, 4 * n + 1, ux, uy))
        dn.wait_recv()
        wx, wy = across(i, bx, by, 2)
        f2 = send(block(i, wx, wy, 1), block(i, wx, wy, 1), b_send.at[i, n, 3], b_recv.at[i, n, 3], to(lo))
        sib.append(hand(i, 4 * n + 2, wx, wy))
        return f1, f2

    last = [[], []]
    for i in range(2):
        last[i].append(relay(i, 0))
    for i in range(2):
        for f in fwd[i]:
            f.wait_recv()
        bx, by = along(i, x, y, 3)
        b[i].append(second(i, 3, bx, by))
    for n in range(1, 4):
        for i in range(2):
            last[i].append(relay(i, n))
    for n in range(4):
        for i in range(2):
            for f in last[i][n]:
                f.wait_recv()
            bx, by = along(i, x, y, n)
            ox, oy = across(i, bx, by, 3)
            sib.append(hand(i, 4 * n + 3, ox, oy))
    for c in qc:
        c.wait_recv()
    for c in sib:
        c.wait_recv()
    for c in sent:
        c.wait_send()


def gather(q, k, v):
    dma = pltpu.SemaphoreType.DMA
    return pl.pallas_call(
        gather_kernel,
        out_shape=(
            jax.ShapeDtypeStruct((PEERS, ROWS, 256), jnp.bfloat16),
            jax.ShapeDtypeStruct((2, 4, 4, 4 * ROWS, D), jnp.bfloat16),
            jax.ShapeDtypeStruct((2, 4, 4, 4 * ROWS, D), jnp.bfloat16),
        ),
        in_specs=[pl.BlockSpec(memory_space=HBM)] * 3,
        out_specs=[pl.BlockSpec(memory_space=HBM)] * 3,
        scratch_shapes=[
            dma((PEERS,)), dma((PEERS,)), dma((2, 4)), dma((2, 4)), dma((3,)),
            dma((2, 4)), dma((2, 4)), dma((2, 4, 4)), dma((2, 4, 4)), dma((2, 16)), dma((2, 16)),
        ],
        compiler_params=pltpu.CompilerParams(collective_id=0, has_side_effects=True),
        name="gather",
    )(q, k, v)


def return_kernel(o_ref, out_ref, send_sem, recv_sem, l_sem):
    x, y, z, core = coords()
    peers = group_peers(x, y, z, core)
    greet([at(*p) for p in peers])
    me = slot_of(x, z, core)
    there = out_ref.at[:, pl.ds(pl.multiple_of(me * 256, 256), 256)]
    copies = []
    for d, p in zip(range(1, PEERS), peers):
        c = pltpu.make_async_remote_copy(
            src_ref=o_ref.at[slot_of(p[0], p[2], p[3])], dst_ref=there,
            send_sem=send_sem.at[d], recv_sem=recv_sem.at[d],
            device_id=at(*p), device_id_type=MESH)
        c.start()
        copies.append(c)
    own = pltpu.make_async_copy(o_ref.at[me], there, l_sem)
    own.start()
    own.wait()
    for c in copies:
        c.wait_recv()
    for c in copies:
        c.wait_send()


def give_back(o):
    dma = pltpu.SemaphoreType.DMA
    return pl.pallas_call(
        return_kernel,
        out_shape=jax.ShapeDtypeStruct((ROWS, HEADS * D), jnp.bfloat16),
        in_specs=[pl.BlockSpec(memory_space=HBM)],
        out_specs=pl.BlockSpec(memory_space=HBM),
        scratch_shapes=[dma((PEERS,)), dma((PEERS,)), dma],
        compiler_params=pltpu.CompilerParams(collective_id=1, has_side_effects=True),
        name="give_back",
    )(o)


def half_of(ref, loc):
    pair = ref[pl.ds(pl.multiple_of((loc // 2) * ROWS, 16), ROWS), :].astype(jnp.float32)
    return jnp.where(loc % 2 == 1, pair[SPAN:], pair[:SPAN])


def attend_kernel(key_at, run_at, run_pos, norms, q_hbm, k_hbm, v_hbm, o_ref,
                  q_raw, k_raw, v_raw, k_sorted, v_sorted, q_tile, rel, acc, tot, top, out32, sem):
    copies = [pltpu.make_async_copy(src, dst, sem.at[i]) for i, (src, dst) in
              enumerate(((k_hbm, k_raw), (v_hbm, v_raw), (q_hbm, q_raw)))]
    for c in copies:
        c.start()
    for c in copies:
        c.wait()

    @pl.loop(0, RUNS // 2)
    def _(j):
        rows = pl.ds(pl.multiple_of(j * ROWS, 16), ROWS)
        a, b = key_at[2 * j], key_at[2 * j + 1]
        k2 = jnp.concatenate([half_of(k_raw, a), half_of(k_raw, b)], axis=0).astype(jnp.bfloat16)
        k_sorted[rows, :D] = k2
        k_sorted[rows, D:] = k2
        v2 = jnp.concatenate([half_of(v_raw, a), half_of(v_raw, b)], axis=0).astype(jnp.bfloat16)
        v_sorted[rows, :] = v2

    def scores(off, width):
        return lax.dot_general(q_tile[...], k_sorted[pl.ds(pl.multiple_of(off, 128), width), :],
                               (((1,), (1,)), ((), ())), preferred_element_type=jnp.float32)

    def product(p, off, width):
        return jnp.dot(p, v_sorted[pl.ds(pl.multiple_of(off, 128), width), :],
                       preferred_element_type=jnp.float32)

    def seen(off):
        return rel[...] >= off

    def plain(j, masked):
        off = j * KEY_TILE
        parts, total = [], None
        for i in range(KEY_TILE // CHUNK):
            s = scores(off + i * CHUNK, CHUNK)
            for w in range(CHUNK // 128):
                p = jnp.exp2(s[:, w * 128:(w + 1) * 128])
                if masked:
                    p = jnp.where(seen(off + i * CHUNK + w * 128), p, 0.0)
                total = p if total is None else total + p
                parts.append(p.astype(jnp.bfloat16))
        acc[...] += product(jnp.concatenate(parts, axis=1), off, KEY_TILE)
        tot[...] += total

    def guarded(j):
        for i in range(KEY_TILE // CHUNK):
            off = j * KEY_TILE + i * CHUNK
            s = scores(off, CHUNK)
            cols, vis, best = [], [], top[...]
            for w in range(CHUNK // 128):
                see = seen(off + w * 128)
                col = jnp.where(see, s[:, w * 128:(w + 1) * 128], -1e30)
                cols.append(col)
                vis.append(see)
                best = jnp.maximum(best, jnp.max(col, axis=1, keepdims=True))
            fade = jnp.exp2(top[...] - best)
            top[...] = best
            total = tot[...] * fade
            parts = []
            for col, see in zip(cols, vis):
                p = jnp.where(see, jnp.exp2(col - best), 0.0)
                total = total + p
                parts.append(p.astype(jnp.bfloat16))
            tot[...] = total
            acc[...] = acc[...] * fade + product(jnp.concatenate(parts, axis=1), off, CHUNK)

    @pl.loop(0, GROUP_RUNS // TILE_RUNS)
    def _(t):
        scaled, places = [], []
        for r in range(TILE_RUNS):
            loc = run_at[t * TILE_RUNS + r]
            scaled.append(half_of(q_raw, loc) * SCALE)
            first = run_pos[t * TILE_RUNS + r] * SPAN
            places.append(lax.broadcasted_iota(jnp.int32, (SPAN, 128), 0)
                          - lax.broadcasted_iota(jnp.int32, (SPAN, 128), 1) + first)
        whole = jnp.concatenate(scaled, axis=0)
        norm = jnp.float32(0)
        for h in range(HEADS_HERE):
            x = whole[:, h * D:(h + 1) * D]
            hi = x.astype(jnp.bfloat16)
            q_tile[h * TILE_ROWS:(h + 1) * TILE_ROWS, :D] = hi
            q_tile[h * TILE_ROWS:(h + 1) * TILE_ROWS, D:] = (x - hi.astype(jnp.float32)).astype(jnp.bfloat16)
            rel[h * TILE_ROWS:(h + 1) * TILE_ROWS, :] = jnp.concatenate(places, axis=0)
            norm = jnp.maximum(norm, jnp.max(jnp.sum(x * x, axis=1, keepdims=True)))
        acc[...] = jnp.zeros_like(acc)
        tot[...] = jnp.zeros_like(tot)
        low = run_pos[t * TILE_RUNS] * SPAN
        high = run_pos[t * TILE_RUNS + TILE_RUNS - 1] * SPAN + SPAN
        full = (low + 1) // KEY_TILE
        count = (high + KEY_TILE - 1) // KEY_TILE
        safe = norm * norms[0] < SAFE * SAFE

        @pl.when(safe)
        def _():
            @pl.loop(0, full)
            def _(j):
                plain(j, False)

            @pl.loop(full, count)
            def _(j):
                plain(j, True)

        @pl.when(jnp.logical_not(safe))
        def _():
            top[...] = jnp.full_like(top, -1e30)

            @pl.loop(0, count)
            def _(j):
                guarded(j)

        done = acc[...] / jnp.sum(tot[...], axis=1, keepdims=True)
        for r in range(TILE_RUNS):
            rows = pl.ds(pl.multiple_of(run_at[t * TILE_RUNS + r] * SPAN, 8), SPAN)
            for h in range(HEADS_HERE):
                out32[rows, h * D:(h + 1) * D] = done[h * TILE_ROWS + r * SPAN:h * TILE_ROWS + (r + 1) * SPAN]

    o_ref[...] = out32[...].astype(jnp.bfloat16)


def attend(key_at, run_at, run_pos, norms, q, k, v):
    smem = pl.BlockSpec(memory_space=pltpu.SMEM)
    rows = PEERS * ROWS
    return pl.pallas_call(
        attend_kernel,
        out_shape=jax.ShapeDtypeStruct((rows, 256), jnp.bfloat16),
        in_specs=[smem] * 4 + [pl.BlockSpec(memory_space=HBM)] * 3,
        out_specs=pl.BlockSpec(memory_space=pltpu.VMEM),
        scratch_shapes=[
            pltpu.VMEM((rows, 256), jnp.bfloat16),
            pltpu.VMEM((SEQ, D), jnp.bfloat16),
            pltpu.VMEM((SEQ, D), jnp.bfloat16),
            pltpu.VMEM((SEQ, 2 * D), jnp.bfloat16),
            pltpu.VMEM((SEQ, D), jnp.bfloat16),
            pltpu.VMEM((M, 2 * D), jnp.bfloat16),
            pltpu.VMEM((M, 128), jnp.int32),
            pltpu.VMEM((M, D), jnp.float32),
            pltpu.VMEM((M, 128), jnp.float32),
            pltpu.VMEM((M, 128), jnp.float32),
            pltpu.VMEM((rows, 256), jnp.float32),
            pltpu.SemaphoreType.DMA((3,)),
        ],
        compiler_params=pltpu.CompilerParams(vmem_limit_bytes=56 << 20),
        name="attend",
    )(key_at, run_at, run_pos, norms, q, k, v)


def on_device(queries, keys, values, positions):
    x, y, z, core = coords()
    squares = jnp.sum(jnp.square(keys.astype(jnp.float32).reshape(ROWS, KV_HEADS, D)), axis=-1)
    news = jnp.concatenate([positions[::SPAN].astype(jnp.float32), jnp.max(squares, axis=0)])
    all_news = lax.all_gather(news, ("outer", "inner"), axis=0, tiled=False)
    qg, kg, vg = gather(queries, keys, values)
    run_index = (all_news[:, :2].astype(jnp.int32) // SPAN).reshape(4, 2, 2, 4, 2, 2)
    norm = jnp.max(lax.dynamic_index_in_dim(all_news[:, 2:], z, 1, keepdims=False))
    places = jnp.arange(RUNS, dtype=jnp.int32)
    at_key = run_index.transpose(2, 0, 1, 4, 3, 5).reshape(RUNS)
    key_at = jnp.sum(jnp.where(at_key[None, :] == places[:, None], places[None, :], 0), axis=1)
    mine = lax.dynamic_index_in_dim(run_index, y, 0, keepdims=False)
    mine = lax.dynamic_index_in_dim(mine, x // 2, 0, keepdims=False)
    mine = mine.transpose(1, 2, 0, 3).reshape(GROUP_RUNS)
    rank = jnp.sum((mine[None, :] < mine[:, None]).astype(jnp.int32), axis=1)
    few = jnp.arange(GROUP_RUNS, dtype=jnp.int32)
    chosen = rank[None, :] == few[:, None]
    run_at = jnp.sum(jnp.where(chosen, few[None, :], 0), axis=1)
    run_pos = jnp.sum(jnp.where(chosen, mine[None, :], 0), axis=1)
    o = attend(key_at, run_at, run_pos, norm.reshape(1),
               qg.reshape(PEERS * ROWS, 256), kg.reshape(SEQ, D), vg.reshape(SEQ, D))
    return give_back(o.reshape(PEERS, ROWS, 256))


def solution(mesh):
    return jax.shard_map(
        on_device,
        mesh=mesh,
        in_specs=(
            P(("outer", "inner"), None),
            P(("outer", "inner"), None),
            P(("outer", "inner"), None),
            P(("outer", "inner")),
        ),
        out_specs=P(("outer", "inner"), None),
        check_vma=False,
    )
```

```python
import functools
import jax
import jax.numpy as jnp
from jax import lax
from jax.experimental import pallas as pl
from jax.experimental.pallas import tpu as pltpu
from jax.sharding import PartitionSpec as P

HEADS = 32
KV_HEADS = 4
D = 128
SPAN = 56
SEQ = 14336
RUNS = SEQ // SPAN
ROWS = 112
KROWS = 128
PEERS = 16
MESH = pl.DeviceIdType.MESH
LOG2E = 1.4426950408889634
SCALE = D ** -0.5 * LOG2E
HBM = pl.ANY
KEY_TILE = 2048
PIECE = 512
PREP = 8
CHUNK = 256
TILE_RUNS = 4
HEADS_HERE = 2
TILE_ROWS = TILE_RUNS * SPAN
M = HEADS_HERE * TILE_ROWS
GROUP_RUNS = 2 * PEERS
SAFE = 90.0


def coords():
    outer, inner = lax.axis_index("outer"), lax.axis_index("inner")
    y, xh, core = outer // 4, (outer // 2) % 2, outer % 2
    return xh * 2 + inner % 2, y, inner // 2, core


def at(x, y, z, core):
    return ((y * 4 + (x // 2) * 2 + core), z * 2 + x % 2)


def greet(devices):
    barrier = pltpu.get_barrier_semaphore()
    for device in devices:
        pl.semaphore_signal(barrier, inc=1, device_id=device, device_id_type=MESH)
    pl.semaphore_wait(barrier, len(devices))


def group_peers(x, y, z, core):
    peers = []
    for d in range(1, PEERS):
        zz = (z + d // 4) % 4
        xx = (x // 2) * 2 + (x % 2 + (d // 2) % 2) % 2
        cc = (core + d % 2) % 2
        peers.append((xx, y, zz, cc))
    return peers


def slot_of(x, z, core):
    return z * 4 + (x % 2) * 2 + core


def gather_kernel(q_ref, k_ref, v_ref, news_ref, qg_ref, kg_ref, vg_ref,
                  q_send, q_recv, z_send, z_recv, l_sem,
                  a_send, a_recv, b_send, b_recv, s_send, s_recv):
    x, y, z, core = coords()
    xr, xl, xo = (x + 1) % 4, (x + 3) % 4, (x + 2) % 4
    yr, yl, yo = (y + 1) % 4, (y + 3) % 4, (y + 2) % 4
    peers = group_peers(x, y, z, core)
    far_x = (x // 2) * 2 + (x + 1) % 2
    other_x = jnp.where(far_x == xr, xl, xr)
    greet([at(*p) for p in peers]
          + [at(other_x, y, z, core), at(x, yr, z, core), at(x, yl, z, core)])

    sent = []

    def send(src, dst, ssem, rsem, to):
        c = pltpu.make_async_remote_copy(
            src_ref=src, dst_ref=dst, send_sem=ssem, recv_sem=rsem,
            device_id=at(*to), device_id_type=MESH)
        c.start()
        sent.append(c)
        return c

    arrays = ((k_ref, kg_ref), (v_ref, vg_ref))
    deep = (KROWS, ROWS)
    def slot(i, rows, start=0):
        return arrays[i][1].at[core, y, x, pl.ds(pl.multiple_of(z * deep[i] + start, 16), rows), :]

    def columns(i, head):
        return arrays[i][0].at[:, pl.ds(pl.multiple_of(head * D, D), D)]

    zc, lc = [], []
    for d in range(1, 4):
        zz = (z + d) % 4
        for i in range(2):
            zc.append(send(columns(i, zz), slot(i, ROWS), z_send.at[i, d], z_recv.at[i, d], (x, y, zz, core)))
        zc.append(send(news_ref, slot(0, KROWS - ROWS, ROWS), z_send.at[2, d], z_recv.at[2, d], (x, y, zz, core)))
    for i, (src, dst) in enumerate(((columns(0, z), slot(0, ROWS)), (columns(1, z), slot(1, ROWS)),
                                    (news_ref, slot(0, KROWS - ROWS, ROWS)))):
        c = pltpu.make_async_copy(src, dst, l_sem.at[i])
        c.start()
        lc.append(c)
    me = slot_of(x, z, core)
    qc = []
    for d, p in zip(range(1, PEERS), peers):
        t = slot_of(p[0], p[2], p[3])
        qc.append(send(q_ref.at[:, pl.ds(pl.multiple_of(t * 256, 256), 256)],
                       qg_ref.at[me], q_send.at[d], q_recv.at[d], p))
    c = pltpu.make_async_copy(q_ref.at[:, pl.ds(pl.multiple_of(me * 256, 256), 256)],
                              qg_ref.at[me], l_sem.at[3])
    c.start()
    lc.append(c)
    for c in zc:
        c.wait_recv()
    for c in lc:
        c.wait()

    def block(i, bx, by, h=None):
        ref, half = arrays[i][1], 2 * deep[i]
        if h is None:
            return ref.at[core, by, bx]
        return ref.at[core, by, bx, pl.ds(h * half, half), :]

    sibling = (x, y, z, 1 - core)
    ring = (((xl, y), (xr, y)), ((x, yl), (x, yr)))
    cross = (((x, yl), (x, yr)), ((xl, y), (xr, y)))

    def to(pos):
        return (pos[0], pos[1], z, core)

    def hand(i, n, bx, by):
        ref = block(i, bx, by)
        return send(ref, ref, s_send.at[i, n], s_recv.at[i, n], sibling)

    sib = []

    def first(i):
        ref = block(i, x, y)
        lo, hi = ring[i]
        up = send(ref, ref, a_send.at[i, 0], a_recv.at[i, 0], to(hi))
        dn = send(ref, ref, a_send.at[i, 1], a_recv.at[i, 1], to(lo))
        return up, dn

    def second(i, n, bx, by):
        ref = block(i, bx, by)
        lo, hi = cross[i]
        up = send(ref, ref, b_send.at[i, n, 0], b_recv.at[i, n, 0], to(hi))
        dn = send(ref, ref, b_send.at[i, n, 1], b_recv.at[i, n, 1], to(lo))
        sib.append(hand(i, 4 * n, bx, by))
        return up, dn

    def along(i, bx, by, n):
        if i == 0:
            return ((bx, by), (xl, by), (xr, by), (xo, by))[n]
        return ((bx, by), (bx, yl), (bx, yr), (bx, yo))[n]

    def across(i, bx, by, n):
        if i == 0:
            return ((bx, by), (bx, yl), (bx, yr), (bx, yo))[n]
        return ((bx, by), (xl, by), (xr, by), (xo, by))[n]

    a = [first(0), first(1)]
    b = [[second(0, 0, x, y)], [second(1, 0, x, y)]]
    fwd = [None, None]
    for i in range(2):
        up, dn = a[i]
        lo, hi = ring[i]
        up.wait_recv()
        bx, by = along(i, x, y, 1)
        f1 = send(block(i, bx, by, 0), block(i, bx, by, 0), a_send.at[i, 2], a_recv.at[i, 2], to(hi))
        dn.wait_recv()
        cx, cy = along(i, x, y, 2)
        f2 = send(block(i, cx, cy, 1), block(i, cx, cy, 1), a_send.at[i, 3], a_recv.at[i, 3], to(lo))
        fwd[i] = (f1, f2)
        b[i].append(second(i, 1, bx, by))
        b[i].append(second(i, 2, cx, cy))

    def relay(i, n):
        bx, by = along(i, x, y, n)
        up, dn = b[i][n]
        lo, hi = cross[i]
        up.wait_recv()
        ux, uy = across(i, bx, by, 1)
        f1 = send(block(i, ux, uy, 0), block(i, ux, uy, 0), b_send.at[i, n, 2], b_recv.at[i, n, 2], to(hi))
        sib.append(hand(i, 4 * n + 1, ux, uy))
        dn.wait_recv()
        wx, wy = across(i, bx, by, 2)
        f2 = send(block(i, wx, wy, 1), block(i, wx, wy, 1), b_send.at[i, n, 3], b_recv.at[i, n, 3], to(lo))
        sib.append(hand(i, 4 * n + 2, wx, wy))
        return f1, f2

    last = [[], []]
    for i in range(2):
        last[i].append(relay(i, 0))
    for i in range(2):
        for f in fwd[i]:
            f.wait_recv()
        bx, by = along(i, x, y, 3)
        b[i].append(second(i, 3, bx, by))
    for n in range(1, 4):
        for i in range(2):
            last[i].append(relay(i, n))
    for n in range(4):
        for i in range(2):
            for f in last[i][n]:
                f.wait_recv()
            bx, by = along(i, x, y, n)
            ox, oy = across(i, bx, by, 3)
            sib.append(hand(i, 4 * n + 3, ox, oy))
    for c in qc:
        c.wait_recv()
    for c in sib:
        c.wait_recv()
    for c in sent:
        c.wait_send()


def gather(q, k, v, news):
    dma = pltpu.SemaphoreType.DMA
    return pl.pallas_call(
        gather_kernel,
        out_shape=(
            jax.ShapeDtypeStruct((PEERS, ROWS, 256), jnp.bfloat16),
            jax.ShapeDtypeStruct((2, 4, 4, 4 * KROWS, D), jnp.bfloat16),
            jax.ShapeDtypeStruct((2, 4, 4, 4 * ROWS, D), jnp.bfloat16),
        ),
        in_specs=[pl.BlockSpec(memory_space=HBM)] * 4,
        out_specs=[pl.BlockSpec(memory_space=HBM)] * 3,
        scratch_shapes=[
            dma((PEERS,)), dma((PEERS,)), dma((3, 4)), dma((3, 4)), dma((4,)),
            dma((2, 4)), dma((2, 4)), dma((2, 4, 4)), dma((2, 4, 4)), dma((2, 16)), dma((2, 16)),
        ],
        compiler_params=pltpu.CompilerParams(collective_id=0, has_side_effects=True),
        name="gather",
    )(q, k, v, news)


def return_kernel(o_ref, out_ref, send_sem, recv_sem, l_sem):
    x, y, z, core = coords()
    peers = group_peers(x, y, z, core)
    greet([at(*p) for p in peers])
    me = slot_of(x, z, core)
    there = out_ref.at[:, pl.ds(pl.multiple_of(me * 256, 256), 256)]
    copies = []
    for d, p in zip(range(1, PEERS), peers):
        c = pltpu.make_async_remote_copy(
            src_ref=o_ref.at[slot_of(p[0], p[2], p[3])], dst_ref=there,
            send_sem=send_sem.at[d], recv_sem=recv_sem.at[d],
            device_id=at(*p), device_id_type=MESH)
        c.start()
        copies.append(c)
    own = pltpu.make_async_copy(o_ref.at[me], there, l_sem)
    own.start()
    own.wait()
    for c in copies:
        c.wait_recv()
    for c in copies:
        c.wait_send()


def give_back(o):
    dma = pltpu.SemaphoreType.DMA
    return pl.pallas_call(
        return_kernel,
        out_shape=jax.ShapeDtypeStruct((ROWS, HEADS * D), jnp.bfloat16),
        in_specs=[pl.BlockSpec(memory_space=HBM)],
        out_specs=pl.BlockSpec(memory_space=HBM),
        scratch_shapes=[dma((PEERS,)), dma((PEERS,)), dma],
        compiler_params=pltpu.CompilerParams(collective_id=1, has_side_effects=True),
        name="give_back",
    )(o)


def half_of(ref, loc, stride=ROWS):
    pair = ref[pl.ds(pl.multiple_of((loc // 2) * stride, 16), ROWS), :].astype(jnp.float32)
    return jnp.where(loc % 2 == 1, pair[SPAN:], pair[:SPAN])


def attend_kernel(run_index, spot, q_hbm, k_hbm, v_hbm, o_ref,
                  q_raw, k_raw, v_raw, k_sorted, v_sorted, q_tile, rel, acc, tot, top, out32,
                  key_at, own, run_at, run_pos, sem):
    copies = [pltpu.make_async_copy(src, dst, sem.at[i]) for i, (src, dst) in
              enumerate(((k_hbm, k_raw), (v_hbm, v_raw), (q_hbm, q_raw)))]
    for c in copies:
        c.start()

    for p in range(RUNS):
        own[p] = -1
    for loc in range(RUNS):
        key_at[run_index[loc]] = loc
    for i in range(GROUP_RUNS):
        z, x_lo, core, half = i // 8, (i // 4) % 2, (i // 2) % 2, i % 2
        loc = (core * 4 + spot[0]) * 32 + (spot[1] * 2 + x_lo) * 8 + z * 2 + half
        own[run_index[loc]] = i
    n = jnp.int32(0)
    for p in range(RUNS):
        who = own[p]
        run_at[n] = who
        run_pos[n] = p
        n = n + jnp.where(who >= 0, 1, 0)
    for c in copies:
        c.wait()

    @pl.loop(0, RUNS // 2 // PREP)
    def _(step):
        for i in range(PREP):
            j = step * PREP + i
            rows = pl.ds(pl.multiple_of(j * ROWS, 16), ROWS)
            a, b = key_at[2 * j], key_at[2 * j + 1]
            k2 = jnp.concatenate([half_of(k_raw, a, KROWS), half_of(k_raw, b, KROWS)], axis=0).astype(jnp.bfloat16)
            k_sorted[rows, :] = k2
            v2 = jnp.concatenate([half_of(v_raw, a), half_of(v_raw, b)], axis=0).astype(jnp.bfloat16)
            v_sorted[rows, :] = v2

    ones = jnp.ones((D, D), jnp.bfloat16)
    longest = None
    for i in range(SEQ // 2048):
        keys = k_sorted[i * 2048:(i + 1) * 2048, :]
        square = jnp.dot(keys * keys, ones, preferred_element_type=jnp.float32)
        square = jnp.max(square, axis=0, keepdims=True)
        longest = square if longest is None else jnp.maximum(longest, square)
    key_norm = jnp.max(longest) * 1.01

    def scores(off, width):
        return lax.dot_general(q_tile[...], k_sorted[pl.ds(pl.multiple_of(off, 128), width), :],
                               (((1,), (1,)), ((), ())), preferred_element_type=jnp.float32) * SCALE

    def product(p, off, width):
        return jnp.dot(p, v_sorted[pl.ds(pl.multiple_of(off, 128), width), :],
                       preferred_element_type=jnp.float32)

    def seen(off):
        see = rel[...] >= off
        return jnp.concatenate([see] * HEADS_HERE, axis=0)

    def plain(off, width, masked):
        parts, total = [], None
        for i in range(width // CHUNK):
            s = scores(off + i * CHUNK, CHUNK)
            for w in range(CHUNK // 128):
                p = jnp.exp2(s[:, w * 128:(w + 1) * 128])
                if masked:
                    p = jnp.where(seen(off + i * CHUNK + w * 128), p, 0.0)
                total = p if total is None else total + p
                parts.append(p.astype(jnp.bfloat16))
        acc[...] += product(jnp.concatenate(parts, axis=1), off, width)
        tot[...] += total

    def guarded(off):
        s = scores(off, CHUNK)
        cols, vis, best = [], [], top[...]
        for w in range(CHUNK // 128):
            see = seen(off + w * 128)
            col = jnp.where(see, s[:, w * 128:(w + 1) * 128], -1e30)
            cols.append(col)
            vis.append(see)
            best = jnp.maximum(best, jnp.max(col, axis=1, keepdims=True))
        fade = jnp.exp2(top[...] - best)
        top[...] = best
        total = tot[...] * fade
        parts = []
        for col, see in zip(cols, vis):
            p = jnp.where(see, jnp.exp2(col - best), 0.0)
            total = total + p
            parts.append(p.astype(jnp.bfloat16))
        tot[...] = total
        acc[...] = acc[...] * fade + product(jnp.concatenate(parts, axis=1), off, CHUNK)

    @pl.loop(0, GROUP_RUNS // TILE_RUNS)
    def _(t):
        scaled, places = [], []
        for r in range(TILE_RUNS):
            loc = run_at[t * TILE_RUNS + r]
            scaled.append(half_of(q_raw, loc))
            first = run_pos[t * TILE_RUNS + r] * SPAN
            places.append(lax.broadcasted_iota(jnp.int32, (SPAN, 128), 0)
                          - lax.broadcasted_iota(jnp.int32, (SPAN, 128), 1) + first)
        whole = jnp.concatenate(scaled, axis=0)
        norm = jnp.float32(0)
        for h in range(HEADS_HERE):
            x = whole[:, h * D:(h + 1) * D]
            q_tile[h * TILE_ROWS:(h + 1) * TILE_ROWS, :] = x.astype(jnp.bfloat16)
            norm = jnp.maximum(norm, jnp.max(jnp.sum(x * x, axis=1, keepdims=True)))
        rel[...] = jnp.concatenate(places, axis=0)
        acc[...] = jnp.zeros_like(acc)
        tot[...] = jnp.zeros_like(tot)
        low = run_pos[t * TILE_RUNS] * SPAN
        high = run_pos[t * TILE_RUNS + TILE_RUNS - 1] * SPAN + SPAN
        full = (low + 1) // KEY_TILE
        pieces = (high + PIECE - 1) // PIECE
        many = KEY_TILE // PIECE
        masked = full + jnp.maximum(pieces - full * many - many, 0) // many
        left = pieces - masked * many
        safe = norm * key_norm * (SCALE * SCALE) < SAFE * SAFE

        @pl.when(safe)
        def _():
            @pl.loop(0, full)
            def _(j):
                plain(j * KEY_TILE, KEY_TILE, False)

            @pl.loop(full, masked)
            def _(j):
                plain(j * KEY_TILE, KEY_TILE, True)

            for n in range(1, 2 * many):
                @pl.when(left == n)
                def _():
                    plain(masked * KEY_TILE, n * PIECE, True)

        @pl.when(jnp.logical_not(safe))
        def _():
            top[...] = jnp.full_like(top, -1e30)

            @pl.loop(0, (high + CHUNK - 1) // CHUNK)
            def _(j):
                guarded(j * CHUNK)

        done = acc[...] / jnp.sum(tot[...], axis=1, keepdims=True)
        for r in range(TILE_RUNS):
            rows = pl.ds(pl.multiple_of(run_at[t * TILE_RUNS + r] * SPAN, 8), SPAN)
            for h in range(HEADS_HERE):
                out32[rows, h * D:(h + 1) * D] = done[h * TILE_ROWS + r * SPAN:h * TILE_ROWS + (r + 1) * SPAN]

    o_ref[...] = out32[...].astype(jnp.bfloat16)


def attend(run_index, spot, q, k, v):
    smem = pl.BlockSpec(memory_space=pltpu.SMEM)
    rows = PEERS * ROWS
    return pl.pallas_call(
        attend_kernel,
        out_shape=jax.ShapeDtypeStruct((rows, 256), jnp.bfloat16),
        in_specs=[smem] * 2 + [pl.BlockSpec(memory_space=HBM)] * 3,
        out_specs=pl.BlockSpec(memory_space=pltpu.VMEM),
        scratch_shapes=[
            pltpu.VMEM((rows, 256), jnp.bfloat16),
            pltpu.VMEM((RUNS // 2 * KROWS, D), jnp.bfloat16),
            pltpu.VMEM((SEQ, D), jnp.bfloat16),
            pltpu.VMEM((SEQ, D), jnp.bfloat16),
            pltpu.VMEM((SEQ, D), jnp.bfloat16),
            pltpu.VMEM((M, D), jnp.bfloat16),
            pltpu.VMEM((TILE_ROWS, 128), jnp.int32),
            pltpu.VMEM((M, D), jnp.float32),
            pltpu.VMEM((M, 128), jnp.float32),
            pltpu.VMEM((M, 128), jnp.float32),
            pltpu.VMEM((rows, 256), jnp.float32),
            pltpu.SMEM((RUNS,), jnp.int32),
            pltpu.SMEM((RUNS,), jnp.int32),
            pltpu.SMEM((GROUP_RUNS + 1,), jnp.int32),
            pltpu.SMEM((GROUP_RUNS + 1,), jnp.int32),
            pltpu.SemaphoreType.DMA((3,)),
        ],
        compiler_params=pltpu.CompilerParams(vmem_limit_bytes=56 << 20),
        name="attend",
    )(run_index, spot, q, k, v)


def on_device(queries, keys, values, positions):
    x, y, z, core = coords()
    runs = (positions[::SPAN] // SPAN).astype(jnp.bfloat16)
    news = jnp.broadcast_to(jnp.pad(runs, (0, D - 2)), (KROWS - ROWS, D))
    qg, kg, vg = gather(queries, keys, values, news)
    run_index = kg.reshape(RUNS // 2, KROWS, D)[:, ROWS, :2].astype(jnp.int32).reshape(RUNS)
    spot = jnp.stack([y, x // 2]).astype(jnp.int32)
    o = attend(run_index, spot, qg.reshape(PEERS * ROWS, 256),
               kg.reshape(RUNS // 2 * KROWS, D), vg.reshape(SEQ, D))
    return give_back(o.reshape(PEERS, ROWS, 256))


def solution(mesh):
    return jax.shard_map(
        on_device,
        mesh=mesh,
        in_specs=(
            P(("outer", "inner"), None),
            P(("outer", "inner"), None),
            P(("outer", "inner"), None),
            P(("outer", "inner")),
        ),
        out_specs=P(("outer", "inner"), None),
        check_vma=False,
    )
```

```python
import functools
import jax
import jax.numpy as jnp
from jax import lax
from jax.experimental import pallas as pl
from jax.experimental.pallas import tpu as pltpu
from jax.sharding import PartitionSpec as P

HEADS = 32
KV_HEADS = 4
D = 128
SPAN = 56
SEQ = 14336
RUNS = SEQ // SPAN
ROWS = 112
KROWS = 128
PEERS = 16
MESH = pl.DeviceIdType.MESH
LOG2E = 1.4426950408889634
SCALE = D ** -0.5 * LOG2E
HBM = pl.ANY
BLOCK = 512
TOGETHER = 16
PREP = 8
SPLIT = 4
CHUNK = 256
TILE_RUNS = 4
GROUP_RUNS = 2 * PEERS
TILES = GROUP_RUNS // TILE_RUNS
HEADS_HERE = 2
TILE_ROWS = TILE_RUNS * SPAN
M = HEADS_HERE * TILE_ROWS
SAFE = 90.0


def coords():
    outer, inner = lax.axis_index("outer"), lax.axis_index("inner")
    y, xh, core = outer // 4, (outer // 2) % 2, outer % 2
    return xh * 2 + inner % 2, y, inner // 2, core


def at(x, y, z, core):
    return ((y * 4 + (x // 2) * 2 + core), z * 2 + x % 2)


def greet(devices):
    barrier = pltpu.get_barrier_semaphore()
    for device in devices:
        pl.semaphore_signal(barrier, inc=1, device_id=device, device_id_type=MESH)
    pl.semaphore_wait(barrier, len(devices))


def group_peers(x, y, z, core):
    peers = []
    for d in range(1, PEERS):
        zz = (z + d // 4) % 4
        xx = (x // 2) * 2 + (x % 2 + (d // 2) % 2) % 2
        cc = (core + d % 2) % 2
        peers.append((xx, y, zz, cc))
    return peers


def slot_of(x, z, core):
    return z * 4 + (x % 2) * 2 + core


def gather_kernel(q_ref, k_ref, v_ref, pos_ref, qg_ref, kg_ref, vg_ref,
                  q_send, q_recv, z_send, z_recv, l_sem,
                  a_send, a_recv, b_send, b_recv, s_send, s_recv, news_ref):
    x, y, z, core = coords()
    xp, xq, xo = x + 1 - 2 * (x % 2), 3 - x, (x + 2) % 4
    yr, yl, yo = (y + 1) % 4, (y + 3) % 4, (y + 2) % 4
    peers = group_peers(x, y, z, core)
    arrays = ((k_ref, kg_ref), (v_ref, vg_ref))
    deep = (KROWS, ROWS)
    def slot(i, rows, start=0):
        return arrays[i][1].at[core, y, x, pl.ds(pl.multiple_of(z * deep[i] + start, 16), rows), :]

    def columns(i, head):
        return arrays[i][0].at[:, pl.ds(pl.multiple_of(head * D, D), D)]

    runs = pos_ref[...].astype(jnp.float32) * (1.0 / SPAN)
    lane = lax.broadcasted_iota(jnp.int32, (1, ROWS), 1)
    later = jnp.sum(jnp.where(lane == SPAN, runs, 0.0), axis=1, keepdims=True)
    news_ref[...] = jnp.zeros_like(news_ref)
    news_ref[:, :ROWS] = jnp.broadcast_to(jnp.where(lane == 1, later, runs), (KROWS - ROWS, ROWS)).astype(jnp.bfloat16)
    me = slot_of(x, z, core)
    lc = []
    for i, (src, dst) in enumerate(((columns(0, z), slot(0, ROWS)), (columns(1, z), slot(1, ROWS)),
                                    (news_ref, slot(0, KROWS - ROWS, ROWS)),
                                    (q_ref.at[:, pl.ds(pl.multiple_of(me * 256, 256), 256)], qg_ref.at[me]))):
        c = pltpu.make_async_copy(src, dst, l_sem.at[i])
        c.start()
        lc.append(c)
    greet([at(*p) for p in peers]
          + [at(xq, y, z, core), at(x, yr, z, core), at(x, yl, z, core)])

    sent = []

    def send(src, dst, ssem, rsem, to):
        c = pltpu.make_async_remote_copy(
            src_ref=src, dst_ref=dst, send_sem=ssem, recv_sem=rsem,
            device_id=at(*to), device_id_type=MESH)
        c.start()
        sent.append(c)
        return c

    def drain(keep):
        while len(sent) > keep:
            sent.pop(0).wait_send()

    zc = []
    for d in range(1, 4):
        zz = (z + d) % 4
        for i in range(2):
            zc.append(send(columns(i, zz), slot(i, ROWS), z_send.at[i, d], z_recv.at[i, d], (x, y, zz, core)))
        zc.append(send(news_ref, slot(0, KROWS - ROWS, ROWS), z_send.at[2, d], z_recv.at[2, d], (x, y, zz, core)))
    qc = []

    def ask(flip):
        for d, p in zip(range(1, PEERS), peers):
            if (d // 2) % 2 == flip:
                t = slot_of(p[0], p[2], p[3])
                qc.append(send(q_ref.at[:, pl.ds(pl.multiple_of(t * 256, 256), 256)],
                               qg_ref.at[me], q_send.at[d], q_recv.at[d], p))

    for c in lc:
        c.wait()
    for c in zc:
        c.wait_recv()
    ask(0)

    def block(i, bx, by, h=None):
        ref, half = arrays[i][1], 2 * deep[i]
        if h is None:
            return ref.at[core, by, bx]
        return ref.at[core, by, bx, pl.ds(h * half, half), :]

    sibling = (x, y, z, 1 - core)
    along_x = ("x", (xp, xq, xo))
    along_y = ("y", (yl, yr, yo))
    axes = ((along_x, along_y), (along_y, along_x))

    def move(axis, bx, by, n):
        if n == 0:
            return bx, by
        return (axis[1][n - 1], by) if axis[0] == "x" else (bx, axis[1][n - 1])

    def spread(i, axis, bx, by, ssem, rsem):
        ref = block(i, bx, by)
        if axis[0] == "x":
            targets = ((xp, y), (xq, y))
        else:
            targets = ((x, yr), (x, yl))
        return [send(ref, ref, ssem.at[k], rsem.at[k], (t[0], t[1], z, core)) for k, t in enumerate(targets)]

    def relay(i, axis, bx, by, got, ssem, rsem, then):
        out = []
        for n in (1, 2):
            got[n - 1].wait_recv()
            ux, uy = move(axis, bx, by, n)
            if axis[0] == "y":
                ref, to = block(i, ux, uy, n - 1), (x, (yr, yl)[n - 1], z, core)
                out.append(send(ref, ref, ssem.at[n + 1], rsem.at[n + 1], to))
            elif n == 1:
                ref = block(i, ux, uy)
                out.append(send(ref, ref, ssem.at[2], rsem.at[2], (xq, y, z, core)))
            then(n, ux, uy)
        return out

    sib = []

    def hand(i, n, bx, by):
        ref = block(i, bx, by)
        sib.append(send(ref, ref, s_send.at[i, n], s_recv.at[i, n], sibling))

    second = [[None] * 4, [None] * 4]

    def start_second(i, n):
        bx, by = move(axes[i][0], x, y, n)
        second[i][n] = spread(i, axes[i][1], bx, by, b_send.at[i, n], b_recv.at[i, n])
        hand(i, 4 * n, bx, by)

    first = [spread(i, axes[i][0], x, y, a_send.at[i], a_recv.at[i]) for i in range(2)]
    for i in range(2):
        start_second(i, 0)
    far = [relay(i, axes[i][0], x, y, first[i], a_send.at[i], a_recv.at[i],
                 lambda n, ux, uy, i=i: start_second(i, n)) for i in range(2)]
    ask(1)
    last = [[None] * 4, [None] * 4]

    def relay_second(i, n):
        bx, by = move(axes[i][0], x, y, n)
        last[i][n] = relay(i, axes[i][1], bx, by, second[i][n], b_send.at[i, n], b_recv.at[i, n],
                           lambda m, ux, uy: hand(i, 4 * n + m, ux, uy))

    drain(24)
    for i in range(2):
        relay_second(i, 0)
    for i in range(2):
        for c in far[i]:
            c.wait_recv()
        start_second(i, 3)
    for n in range(1, 4):
        drain(24)
        for i in range(2):
            relay_second(i, n)
    for n in range(4):
        for i in range(2):
            drain(16)
            for c in last[i][n]:
                c.wait_recv()
            hand(i, 4 * n + 3, *move(axes[i][1], *move(axes[i][0], x, y, n), 3))
    for c in qc:
        c.wait_recv()
    for c in sib:
        c.wait_recv()
    drain(0)


def gather(q, k, v, positions):
    dma = pltpu.SemaphoreType.DMA
    return pl.pallas_call(
        gather_kernel,
        out_shape=(
            jax.ShapeDtypeStruct((PEERS, ROWS, 256), jnp.bfloat16),
            jax.ShapeDtypeStruct((2, 4, 4, 4 * KROWS, D), jnp.bfloat16),
            jax.ShapeDtypeStruct((2, 4, 4, 4 * ROWS, D), jnp.bfloat16),
        ),
        in_specs=[pl.BlockSpec(memory_space=HBM)] * 3 + [pl.BlockSpec(memory_space=pltpu.VMEM)],
        out_specs=[pl.BlockSpec(memory_space=HBM)] * 3,
        scratch_shapes=[
            dma((PEERS,)), dma((PEERS,)), dma((3, 4)), dma((3, 4)), dma((4,)),
            dma((2, 4)), dma((2, 4)), dma((2, 4, 4)), dma((2, 4, 4)), dma((2, 16)), dma((2, 16)),
            pltpu.VMEM((KROWS - ROWS, D), jnp.bfloat16),
        ],
        compiler_params=pltpu.CompilerParams(collective_id=0, has_side_effects=True),
        name="gather",
    )(q, k, v, positions)


def return_kernel(o_ref, out_ref, send_sem, recv_sem, l_sem):
    x, y, z, core = coords()
    peers = group_peers(x, y, z, core)
    me = slot_of(x, z, core)
    there = out_ref.at[:, pl.ds(pl.multiple_of(me * 256, 256), 256)]
    own = pltpu.make_async_copy(o_ref.at[me], there, l_sem)
    own.start()
    greet([at(*p) for p in peers])
    copies = []
    for d, p in zip(range(1, PEERS), peers):
        c = pltpu.make_async_remote_copy(
            src_ref=o_ref.at[slot_of(p[0], p[2], p[3])], dst_ref=there,
            send_sem=send_sem.at[d], recv_sem=recv_sem.at[d],
            device_id=at(*p), device_id_type=MESH)
        c.start()
        copies.append(c)
    own.wait()
    for c in copies:
        c.wait_recv()
    for c in copies:
        c.wait_send()


def give_back(o):
    dma = pltpu.SemaphoreType.DMA
    return pl.pallas_call(
        return_kernel,
        out_shape=jax.ShapeDtypeStruct((ROWS, HEADS * D), jnp.bfloat16),
        in_specs=[pl.BlockSpec(memory_space=HBM)],
        out_specs=pl.BlockSpec(memory_space=HBM),
        scratch_shapes=[dma((PEERS,)), dma((PEERS,)), dma],
        compiler_params=pltpu.CompilerParams(collective_id=1, has_side_effects=True),
        name="give_back",
    )(o)


def half_of(ref, loc, stride=ROWS):
    pair = ref[pl.ds(pl.multiple_of((loc // 2) * stride, 16), ROWS), :].astype(jnp.float32)
    return jnp.where(loc % 2 == 1, pair[SPAN:], pair[:SPAN])


def attend_kernel(run_index, q_hbm, k_hbm, v_hbm, o_ref,
                  q_raw, k_raw, v_raw, k_sorted, v_sorted, q_tile, rel, acc, tot, top, weights, lately, part, part_tot, out32,
                  key_at, own, run_at, run_pos, blocks, sem):
    copies = []
    for src, dst in ((q_hbm, q_raw), (k_hbm, k_raw), (v_hbm, v_raw)):
        size = src.shape[0] // SPLIT
        for i in range(SPLIT):
            rows = pl.ds(i * size, size)
            copies.append(pltpu.make_async_copy(src.at[rows, :], dst.at[rows, :], sem.at[len(copies)]))
            copies[-1].start()

    my_x, my_y, _, _ = coords()
    for p in range(RUNS):
        own[p] = -1
    for loc in range(RUNS):
        key_at[run_index[loc]] = loc
    for i in range(GROUP_RUNS):
        z, x_lo, core, half = i // 8, (i // 4) % 2, (i // 2) % 2, i % 2
        loc = (core * 4 + my_y) * 32 + (my_x // 2 * 2 + x_lo) * 8 + z * 2 + half
        own[run_index[loc]] = i
    n = jnp.int32(0)
    for p in range(RUNS):
        who = own[p]
        run_at[n] = who
        run_pos[n] = p
        n = n + jnp.where(who >= 0, 1, 0)
    for c in copies:
        c.wait()

    @pl.loop(0, RUNS // 2 // PREP)
    def _(step):
        for i in range(PREP):
            j = step * PREP + i
            rows = pl.ds(pl.multiple_of(j * ROWS, 16), ROWS)
            a, b = key_at[2 * j], key_at[2 * j + 1]
            k2 = jnp.concatenate([half_of(k_raw, a, KROWS), half_of(k_raw, b, KROWS)], axis=0).astype(jnp.bfloat16)
            k_sorted[rows, :] = k2
            v2 = jnp.concatenate([half_of(v_raw, a), half_of(v_raw, b)], axis=0).astype(jnp.bfloat16)
            v_sorted[rows, :] = v2

    ones = jnp.ones((D, D), jnp.bfloat16)
    longest = None
    for i in range(SEQ // 2048):
        keys = k_sorted[i * 2048:(i + 1) * 2048, :]
        square = jnp.dot(keys * keys, ones, preferred_element_type=jnp.float32)
        square = jnp.max(square, axis=0, keepdims=True)
        longest = square if longest is None else jnp.maximum(longest, square)
    key_norm = jnp.max(longest) * 1.01

    longest = None
    for t in range(TILES):
        scaled = [half_of(q_raw, run_at[t * TILE_RUNS + r]) for r in range(TILE_RUNS)]
        whole = jnp.concatenate(scaled, axis=0).astype(jnp.bfloat16)
        for h in range(HEADS_HERE):
            x = whole[:, h * D:(h + 1) * D]
            q_tile[t * M + h * TILE_ROWS:t * M + (h + 1) * TILE_ROWS, :] = x
            square = jnp.dot(x * x, ones, preferred_element_type=jnp.float32)
            square = jnp.max(square, axis=0, keepdims=True)
            longest = square if longest is None else jnp.maximum(longest, square)
    query_norm = jnp.max(longest) * 1.01
    safe = query_norm * key_norm * (SCALE * SCALE) < SAFE * SAFE
    acc[...] = jnp.zeros_like(acc)
    tot[...] = jnp.zeros_like(tot)

    def rows_of(t):
        return pl.ds(pl.multiple_of(t * M, M), M)

    def scores(at, off, width):
        return lax.dot_general(q_tile[at, :], k_sorted[pl.ds(pl.multiple_of(off, 128), width), :],
                               (((1,), (1,)), ((), ())), preferred_element_type=jnp.float32) * SCALE

    def product(p, off, width):
        return jnp.dot(p, v_sorted[pl.ds(pl.multiple_of(off, 128), width), :],
                       preferred_element_type=jnp.float32)

    def seen(t, off):
        see = rel[t] >= off
        return jnp.concatenate([see] * HEADS_HERE, axis=0)

    def weigh(t, off, slot):
        at, total = rows_of(t), None
        for i in range(BLOCK // CHUNK):
            s = scores(at, off + i * CHUNK, CHUNK)
            for w in range(0, CHUNK, 128):
                p = jnp.where(seen(t, off + i * CHUNK + w), jnp.exp2(s[:, w:w + 128]), 0.0)
                total = p if total is None else total + p
                weights[slot, :, i * CHUNK + w:i * CHUNK + w + 128] = p.astype(jnp.bfloat16)
        lately[slot] = total

    def guarded(t, off):
        at = rows_of(t)
        s = scores(at, off, CHUNK)
        cols, vis, best = [], [], top[...]
        for w in range(CHUNK // 128):
            see = seen(t, off + w * 128)
            col = jnp.where(see, s[:, w * 128:(w + 1) * 128], -1e30)
            cols.append(col)
            vis.append(see)
            best = jnp.maximum(best, jnp.max(col, axis=1, keepdims=True))
        fade = jnp.exp2(top[...] - best)
        top[...] = best
        total = tot[at, :] * fade
        parts = []
        for col, see in zip(cols, vis):
            p = jnp.where(see, jnp.exp2(col - best), 0.0)
            total = total + p
            parts.append(p.astype(jnp.bfloat16))
        tot[at, :] = total
        acc[at, :] = acc[at, :] * fade + product(jnp.concatenate(parts, axis=1), off, CHUNK)

    count = jnp.int32(0)
    for t in range(TILES):
        for r in range(TILE_RUNS):
            first = run_pos[t * TILE_RUNS + r] * SPAN
            rel[t, r * SPAN:(r + 1) * SPAN, :] = (lax.broadcasted_iota(jnp.int32, (SPAN, 128), 0)
                                                  - lax.broadcasted_iota(jnp.int32, (SPAN, 128), 1) + first)
        high = run_pos[t * TILE_RUNS + TILE_RUNS - 1] * SPAN + SPAN
        blocks[t] = (high + BLOCK - 1) // BLOCK
        count = count + blocks[t]
    blocks[TILES] = 1
    rel[TILES] = jnp.full_like(rel[TILES], -1)
    weights[...] = jnp.zeros_like(weights)
    lately[...] = jnp.zeros_like(lately)

    def following(t, j):
        end = j + 1 >= blocks[t]
        return jnp.minimum(t + jnp.where(end, 1, 0), TILES), jnp.where(end, 0, j + 1)

    @pl.when(safe)
    def _():
        def settle(t, u):
            acc[rows_of(t), :] += part[u]
            tot[rows_of(t), :] += part_tot[u]

        def step(_, state):
            t, j, before, at = state
            tiles = []
            for u in range(TOGETHER):
                out, out_tot = product(weights[(u + 1) % 2], at, BLOCK), lately[(u + 1) % 2]
                if u:
                    same = before == tiles[-1]
                    out = out + jnp.where(same, part[u - 1], 0.0)
                    out_tot = out_tot + jnp.where(same, part_tot[u - 1], 0.0)
                part[u] = out
                part_tot[u] = out_tot
                weigh(t, j * BLOCK, u % 2)
                tiles.append(before)
                before, at = t, j * BLOCK
                t, j = following(t, j)
            for u in range(TOGETHER - 1):
                @pl.when(tiles[u] != tiles[u + 1])
                def _():
                    settle(tiles[u], u)
            settle(tiles[-1], TOGETHER - 1)
            return t, j, before, at

        zero = jnp.int32(0)
        _, _, before, at = lax.fori_loop(0, (count + TOGETHER - 1) // TOGETHER, step,
                                         (zero, zero, zero + TILES, zero))
        part[0] = product(weights[(TOGETHER + 1) % 2], at, BLOCK)
        part_tot[0] = lately[(TOGETHER + 1) % 2]
        settle(before, 0)

    @pl.when(jnp.logical_not(safe))
    def _():
        @pl.loop(0, TILES)
        def _(t):
            top[...] = jnp.full_like(top, -1e30)

            @pl.loop(0, blocks[t] * (BLOCK // CHUNK))
            def _(j):
                guarded(t, j * CHUNK)

    for t in range(TILES):
        rows = slice(t * M, (t + 1) * M)
        done = acc[rows, :] / jnp.sum(tot[rows, :], axis=1, keepdims=True)
        for r in range(TILE_RUNS):
            rows = pl.ds(pl.multiple_of(run_at[t * TILE_RUNS + r] * SPAN, 8), SPAN)
            for h in range(HEADS_HERE):
                out32[rows, h * D:(h + 1) * D] = done[h * TILE_ROWS + r * SPAN:h * TILE_ROWS + (r + 1) * SPAN]

    o_ref[...] = out32[...].astype(jnp.bfloat16)


def attend(run_index, q, k, v):
    smem = pl.BlockSpec(memory_space=pltpu.SMEM)
    rows = PEERS * ROWS
    return pl.pallas_call(
        attend_kernel,
        out_shape=jax.ShapeDtypeStruct((rows, 256), jnp.bfloat16),
        in_specs=[smem] + [pl.BlockSpec(memory_space=HBM)] * 3,
        out_specs=pl.BlockSpec(memory_space=pltpu.VMEM),
        scratch_shapes=[
            pltpu.VMEM((rows, 256), jnp.bfloat16),
            pltpu.VMEM((RUNS // 2 * KROWS, D), jnp.bfloat16),
            pltpu.VMEM((SEQ, D), jnp.bfloat16),
            pltpu.VMEM((SEQ, D), jnp.bfloat16),
            pltpu.VMEM((SEQ, D), jnp.bfloat16),
            pltpu.VMEM((TILES * M + M, D), jnp.bfloat16),
            pltpu.VMEM((TILES + 1, TILE_ROWS, 128), jnp.int32),
            pltpu.VMEM((TILES * M + M, D), jnp.float32),
            pltpu.VMEM((TILES * M + M, 128), jnp.float32),
            pltpu.VMEM((M, 128), jnp.float32),
            pltpu.VMEM((2, M, BLOCK), jnp.bfloat16),
            pltpu.VMEM((2, M, 128), jnp.float32),
            pltpu.VMEM((TOGETHER, M, D), jnp.float32),
            pltpu.VMEM((TOGETHER, M, 128), jnp.float32),
            pltpu.VMEM((rows, 256), jnp.float32),
            pltpu.SMEM((RUNS,), jnp.int32),
            pltpu.SMEM((RUNS,), jnp.int32),
            pltpu.SMEM((GROUP_RUNS + 1,), jnp.int32),
            pltpu.SMEM((GROUP_RUNS + 1,), jnp.int32),
            pltpu.SMEM((TILES + 1,), jnp.int32),
            pltpu.SemaphoreType.DMA((3 * SPLIT,)),
        ],
        compiler_params=pltpu.CompilerParams(vmem_limit_bytes=56 << 20),
        name="attend",
    )(run_index, q, k, v)


def on_device(queries, keys, values, positions):
    qg, kg, vg = gather(queries, keys, values, positions.reshape(1, ROWS))
    run_index = kg.reshape(RUNS // 2, KROWS, D)[:, ROWS, :2].astype(jnp.int32).reshape(RUNS)
    o = attend(run_index, qg.reshape(PEERS * ROWS, 256),
               kg.reshape(RUNS // 2 * KROWS, D), vg.reshape(SEQ, D))
    return give_back(o.reshape(PEERS, ROWS, 256))


def solution(mesh):
    return jax.shard_map(
        on_device,
        mesh=mesh,
        in_specs=(
            P(("outer", "inner"), None),
            P(("outer", "inner"), None),
            P(("outer", "inner"), None),
            P(("outer", "inner")),
        ),
        out_specs=P(("outer", "inner"), None),
        check_vma=False,
    )
```

```python
import functools
import jax
import jax.numpy as jnp
from jax import lax
from jax.experimental import pallas as pl
from jax.experimental.pallas import tpu as pltpu
from jax.sharding import PartitionSpec as P

HEADS = 32
KV_HEADS = 4
D = 128
SPAN = 56
SEQ = 14336
RUNS = SEQ // SPAN
ROWS = 112
KROWS = 128
PEERS = 16
MESH = pl.DeviceIdType.MESH
LOG2E = 1.4426950408889634
SCALE = D ** -0.5 * LOG2E
HBM = pl.ANY
BLOCK = 512
TOGETHER = 16
FEW = 4
PREP = 8
SPLIT = 4
CHUNK = 256
TILE_RUNS = 4
GROUP_RUNS = 2 * PEERS
TILES = GROUP_RUNS // TILE_RUNS
HEADS_HERE = 2
TILE_ROWS = TILE_RUNS * SPAN
M = HEADS_HERE * TILE_ROWS
SAFE = 90.0


def coords():
    outer, inner = lax.axis_index("outer"), lax.axis_index("inner")
    y, xh, core = outer // 4, (outer // 2) % 2, outer % 2
    return xh * 2 + inner % 2, y, inner // 2, core


def at(x, y, z, core):
    return ((y * 4 + (x // 2) * 2 + core), z * 2 + x % 2)


def greet(devices):
    barrier = pltpu.get_barrier_semaphore()
    for device in devices:
        pl.semaphore_signal(barrier, inc=1, device_id=device, device_id_type=MESH)
    pl.semaphore_wait(barrier, len(devices))


def group_peers(x, y, z, core):
    peers = []
    for d in range(1, PEERS):
        zz = (z + d // 4) % 4
        xx = (x // 2) * 2 + (x % 2 + (d // 2) % 2) % 2
        cc = (core + d % 2) % 2
        peers.append((xx, y, zz, cc))
    return peers


def slot_of(x, z, core):
    return z * 4 + (x % 2) * 2 + core


def gather_kernel(q_ref, k_ref, v_ref, pos_ref, qg_ref, kg_ref, vg_ref,
                  q_send, q_recv, z_send, z_recv, l_sem,
                  a_send, a_recv, b_send, b_recv, s_send, s_recv, news_ref):
    x, y, z, core = coords()
    xp, xq, xo = x + 1 - 2 * (x % 2), 3 - x, (x + 2) % 4
    yr, yl, yo = (y + 1) % 4, (y + 3) % 4, (y + 2) % 4
    peers = group_peers(x, y, z, core)
    arrays = ((k_ref, kg_ref), (v_ref, vg_ref))
    deep = (KROWS, ROWS)
    def slot(i, rows, start=0):
        return arrays[i][1].at[core, y, x, pl.ds(pl.multiple_of(z * deep[i] + start, 16), rows), :]

    def columns(i, head):
        return arrays[i][0].at[:, pl.ds(pl.multiple_of(head * D, D), D)]

    runs = pos_ref[...].astype(jnp.float32) * (1.0 / SPAN)
    lane = lax.broadcasted_iota(jnp.int32, (1, ROWS), 1)
    later = jnp.sum(jnp.where(lane == SPAN, runs, 0.0), axis=1, keepdims=True)
    news_ref[...] = jnp.zeros_like(news_ref)
    news_ref[:, :ROWS] = jnp.broadcast_to(jnp.where(lane == 1, later, runs), (KROWS - ROWS, ROWS)).astype(jnp.bfloat16)
    me = slot_of(x, z, core)
    lc = []
    for i, (src, dst) in enumerate(((columns(0, z), slot(0, ROWS)), (columns(1, z), slot(1, ROWS)),
                                    (news_ref, slot(0, KROWS - ROWS, ROWS)),
                                    (q_ref.at[:, pl.ds(pl.multiple_of(me * 256, 256), 256)], qg_ref.at[me]))):
        c = pltpu.make_async_copy(src, dst, l_sem.at[i])
        c.start()
        lc.append(c)
    greet([at(*p) for p in peers]
          + [at(xq, y, z, core), at(xo, y, z, core), at(x, yr, z, core), at(x, yl, z, core), at(x, yo, z, core)])

    sent = []

    def send(src, dst, ssem, rsem, to):
        c = pltpu.make_async_remote_copy(
            src_ref=src, dst_ref=dst, send_sem=ssem, recv_sem=rsem,
            device_id=at(*to), device_id_type=MESH)
        c.start()
        sent.append(c)
        return c

    def drain(keep):
        while len(sent) > keep:
            sent.pop(0).wait_send()

    zc = []
    for d in range(1, 4):
        zz = (z + d) % 4
        for i in range(2):
            zc.append(send(columns(i, zz), slot(i, ROWS), z_send.at[i, d], z_recv.at[i, d], (x, y, zz, core)))
        zc.append(send(news_ref, slot(0, KROWS - ROWS, ROWS), z_send.at[2, d], z_recv.at[2, d], (x, y, zz, core)))
    qc = []

    def ask(flip):
        for d, p in zip(range(1, PEERS), peers):
            if (d // 2) % 2 == flip:
                t = slot_of(p[0], p[2], p[3])
                qc.append(send(q_ref.at[:, pl.ds(pl.multiple_of(t * 256, 256), 256)],
                               qg_ref.at[me], q_send.at[d], q_recv.at[d], p))

    for c in lc:
        c.wait()
    for c in zc:
        c.wait_recv()
    ask(0)

    def block(i, bx, by, h=None):
        ref, half = arrays[i][1], 2 * deep[i]
        if h is None:
            return ref.at[core, by, bx]
        return ref.at[core, by, bx, pl.ds(h * half, half), :]

    sibling = (x, y, z, 1 - core)
    along_x = ("x", (xp, xq, xo))
    along_y = ("y", (yl, yr, yo))
    axes = ((along_x, along_y), (along_y, along_x))

    def move(axis, bx, by, n):
        if n == 0:
            return bx, by
        return (axis[1][n - 1], by) if axis[0] == "x" else (bx, axis[1][n - 1])

    def spread(i, axis, bx, by, ssem, rsem, direct):
        ref = block(i, bx, by)
        targets = ((xp, y), (xq, y), (xo, y)) if axis[0] == "x" else ((x, yr), (x, yl), (x, yo))
        return [send(ref, ref, ssem.at[k], rsem.at[k], (t[0], t[1], z, core))
                for k, t in enumerate(targets[:3 if direct else 2])]

    def relay(i, axis, bx, by, got, ssem, rsem, then):
        out = got[2:]
        for n in (1, 2):
            got[n - 1].wait_recv()
            ux, uy = move(axis, bx, by, n)
            if len(got) == 2 and axis[0] == "y":
                ref, to = block(i, ux, uy, n - 1), (x, (yr, yl)[n - 1], z, core)
                out.append(send(ref, ref, ssem.at[n + 1], rsem.at[n + 1], to))
            elif len(got) == 2 and n == 1:
                ref = block(i, ux, uy)
                out.append(send(ref, ref, ssem.at[2], rsem.at[2], (xq, y, z, core)))
            then(n, ux, uy)
        return out

    sib = []

    def hand(i, n, bx, by):
        ref = block(i, bx, by)
        sib.append(send(ref, ref, s_send.at[i, n], s_recv.at[i, n], sibling))

    second = [[None] * 4, [None] * 4]

    def start_second(i, n):
        bx, by = move(axes[i][0], x, y, n)
        second[i][n] = spread(i, axes[i][1], bx, by, b_send.at[i, n], b_recv.at[i, n], n == 3)
        hand(i, 4 * n, bx, by)

    first = [spread(i, axes[i][0], x, y, a_send.at[i], a_recv.at[i], False) for i in range(2)]
    for i in range(2):
        start_second(i, 0)
    far = [relay(i, axes[i][0], x, y, first[i], a_send.at[i], a_recv.at[i],
                 lambda n, ux, uy, i=i: start_second(i, n)) for i in range(2)]
    ask(1)
    last = [[None] * 4, [None] * 4]

    def relay_second(i, n):
        bx, by = move(axes[i][0], x, y, n)
        last[i][n] = relay(i, axes[i][1], bx, by, second[i][n], b_send.at[i, n], b_recv.at[i, n],
                           lambda m, ux, uy: hand(i, 4 * n + m, ux, uy))

    drain(24)
    for i in range(2):
        relay_second(i, 0)
    for i in range(2):
        for c in far[i]:
            c.wait_recv()
        start_second(i, 3)
    for n in range(1, 4):
        drain(24)
        for i in range(2):
            relay_second(i, n)
    for n in range(4):
        for i in range(2):
            drain(16)
            for c in last[i][n]:
                c.wait_recv()
            hand(i, 4 * n + 3, *move(axes[i][1], *move(axes[i][0], x, y, n), 3))
    for c in qc:
        c.wait_recv()
    for c in sib:
        c.wait_recv()
    drain(0)


def gather(q, k, v, positions):
    dma = pltpu.SemaphoreType.DMA
    return pl.pallas_call(
        gather_kernel,
        out_shape=(
            jax.ShapeDtypeStruct((PEERS, ROWS, 256), jnp.bfloat16),
            jax.ShapeDtypeStruct((2, 4, 4, 4 * KROWS, D), jnp.bfloat16),
            jax.ShapeDtypeStruct((2, 4, 4, 4 * ROWS, D), jnp.bfloat16),
        ),
        in_specs=[pl.BlockSpec(memory_space=HBM)] * 3 + [pl.BlockSpec(memory_space=pltpu.VMEM)],
        out_specs=[pl.BlockSpec(memory_space=HBM)] * 3,
        scratch_shapes=[
            dma((PEERS,)), dma((PEERS,)), dma((3, 4)), dma((3, 4)), dma((4,)),
            dma((2, 4)), dma((2, 4)), dma((2, 4, 4)), dma((2, 4, 4)), dma((2, 16)), dma((2, 16)),
            pltpu.VMEM((KROWS - ROWS, D), jnp.bfloat16),
        ],
        compiler_params=pltpu.CompilerParams(collective_id=0, has_side_effects=True),
        name="gather",
    )(q, k, v, positions)


def return_kernel(o_ref, out_ref, send_sem, recv_sem, l_sem):
    x, y, z, core = coords()
    peers = group_peers(x, y, z, core)
    me = slot_of(x, z, core)
    there = out_ref.at[:, pl.ds(pl.multiple_of(me * 256, 256), 256)]
    own = pltpu.make_async_copy(o_ref.at[me], there, l_sem)
    own.start()
    greet([at(*p) for p in peers])
    copies = []
    for d, p in zip(range(1, PEERS), peers):
        c = pltpu.make_async_remote_copy(
            src_ref=o_ref.at[slot_of(p[0], p[2], p[3])], dst_ref=there,
            send_sem=send_sem.at[d], recv_sem=recv_sem.at[d],
            device_id=at(*p), device_id_type=MESH)
        c.start()
        copies.append(c)
    own.wait()
    for c in copies:
        c.wait_recv()
    for c in copies:
        c.wait_send()


def give_back(o):
    dma = pltpu.SemaphoreType.DMA
    return pl.pallas_call(
        return_kernel,
        out_shape=jax.ShapeDtypeStruct((ROWS, HEADS * D), jnp.bfloat16),
        in_specs=[pl.BlockSpec(memory_space=HBM)],
        out_specs=pl.BlockSpec(memory_space=HBM),
        scratch_shapes=[dma((PEERS,)), dma((PEERS,)), dma],
        compiler_params=pltpu.CompilerParams(collective_id=1, has_side_effects=True),
        name="give_back",
    )(o)


def half_of(ref, loc, stride=ROWS):
    pair = ref[pl.ds(pl.multiple_of((loc // 2) * stride, 16), ROWS), :].astype(jnp.float32)
    return jnp.where(loc % 2 == 1, pair[SPAN:], pair[:SPAN])


def attend_kernel(run_index, q_hbm, k_hbm, v_hbm, o_ref,
                  q_raw, k_raw, v_raw, k_sorted, v_sorted, q_tile, rel, acc, tot, top, weights, lately, part, part_tot, out32,
                  key_at, own, run_at, run_pos, blocks, sem):
    copies = []
    for src, dst in ((q_hbm, q_raw), (k_hbm, k_raw), (v_hbm, v_raw)):
        size = src.shape[0] // SPLIT
        for i in range(SPLIT):
            rows = pl.ds(i * size, size)
            copies.append(pltpu.make_async_copy(src.at[rows, :], dst.at[rows, :], sem.at[len(copies)]))
            copies[-1].start()

    my_x, my_y, _, _ = coords()
    for p in range(RUNS):
        own[p] = -1
    for loc in range(RUNS):
        key_at[run_index[loc]] = loc
    for i in range(GROUP_RUNS):
        z, x_lo, core, half = i // 8, (i // 4) % 2, (i // 2) % 2, i % 2
        loc = (core * 4 + my_y) * 32 + (my_x // 2 * 2 + x_lo) * 8 + z * 2 + half
        own[run_index[loc]] = i
    n = jnp.int32(0)
    for p in range(RUNS):
        who = own[p]
        run_at[n] = who
        run_pos[n] = p
        n = n + jnp.where(who >= 0, 1, 0)
    for c in copies:
        c.wait()

    @pl.loop(0, RUNS // 2 // PREP)
    def _(step):
        for i in range(PREP):
            j = step * PREP + i
            rows = pl.ds(pl.multiple_of(j * ROWS, 16), ROWS)
            a, b = key_at[2 * j], key_at[2 * j + 1]
            k2 = jnp.concatenate([half_of(k_raw, a, KROWS), half_of(k_raw, b, KROWS)], axis=0).astype(jnp.bfloat16)
            k_sorted[rows, :] = k2
            v2 = jnp.concatenate([half_of(v_raw, a), half_of(v_raw, b)], axis=0).astype(jnp.bfloat16)
            v_sorted[rows, :] = v2

    ones = jnp.ones((D, D), jnp.bfloat16)
    longest = None
    for i in range(SEQ // 2048):
        keys = k_sorted[i * 2048:(i + 1) * 2048, :]
        square = jnp.dot(keys * keys, ones, preferred_element_type=jnp.float32)
        square = jnp.max(square, axis=0, keepdims=True)
        longest = square if longest is None else jnp.maximum(longest, square)
    key_norm = jnp.max(longest) * 1.01

    longest = None
    for t in range(TILES):
        scaled = [half_of(q_raw, run_at[t * TILE_RUNS + r]) for r in range(TILE_RUNS)]
        whole = jnp.concatenate(scaled, axis=0).astype(jnp.bfloat16)
        for h in range(HEADS_HERE):
            x = whole[:, h * D:(h + 1) * D]
            q_tile[t * M + h * TILE_ROWS:t * M + (h + 1) * TILE_ROWS, :] = x
            square = jnp.dot(x * x, ones, preferred_element_type=jnp.float32)
            square = jnp.max(square, axis=0, keepdims=True)
            longest = square if longest is None else jnp.maximum(longest, square)
    query_norm = jnp.max(longest) * 1.01
    safe = query_norm * key_norm * (SCALE * SCALE) < SAFE * SAFE
    acc[...] = jnp.zeros_like(acc)
    tot[...] = jnp.zeros_like(tot)

    def rows_of(t):
        return pl.ds(pl.multiple_of(t * M, M), M)

    def scores(at, off, width):
        return lax.dot_general(q_tile[at, :], k_sorted[pl.ds(pl.multiple_of(off, 128), width), :],
                               (((1,), (1,)), ((), ())), preferred_element_type=jnp.float32) * SCALE

    def product(p, off, width):
        return jnp.dot(p, v_sorted[pl.ds(pl.multiple_of(off, 128), width), :],
                       preferred_element_type=jnp.float32)

    def seen(t, off):
        see = rel[t] >= off
        return jnp.concatenate([see] * HEADS_HERE, axis=0)

    def weigh(t, off, slot):
        at, total = rows_of(t), None
        for i in range(BLOCK // CHUNK):
            s = scores(at, off + i * CHUNK, CHUNK)
            for w in range(0, CHUNK, 128):
                p = jnp.where(seen(t, off + i * CHUNK + w), jnp.exp2(s[:, w:w + 128]), 0.0)
                total = p if total is None else total + p
                weights[slot, :, i * CHUNK + w:i * CHUNK + w + 128] = p.astype(jnp.bfloat16)
        lately[slot] = total

    def guarded(t, off):
        at = rows_of(t)
        s = scores(at, off, CHUNK)
        cols, vis, best = [], [], top[...]
        for w in range(CHUNK // 128):
            see = seen(t, off + w * 128)
            col = jnp.where(see, s[:, w * 128:(w + 1) * 128], -1e30)
            cols.append(col)
            vis.append(see)
            best = jnp.maximum(best, jnp.max(col, axis=1, keepdims=True))
        fade = jnp.exp2(top[...] - best)
        top[...] = best
        total = tot[at, :] * fade
        parts = []
        for col, see in zip(cols, vis):
            p = jnp.where(see, jnp.exp2(col - best), 0.0)
            total = total + p
            parts.append(p.astype(jnp.bfloat16))
        tot[at, :] = total
        acc[at, :] = acc[at, :] * fade + product(jnp.concatenate(parts, axis=1), off, CHUNK)

    count = jnp.int32(0)
    for t in range(TILES):
        for r in range(TILE_RUNS):
            first = run_pos[t * TILE_RUNS + r] * SPAN
            rel[t, r * SPAN:(r + 1) * SPAN, :] = (lax.broadcasted_iota(jnp.int32, (SPAN, 128), 0)
                                                  - lax.broadcasted_iota(jnp.int32, (SPAN, 128), 1) + first)
        high = run_pos[t * TILE_RUNS + TILE_RUNS - 1] * SPAN + SPAN
        blocks[t] = (high + BLOCK - 1) // BLOCK
        count = count + blocks[t]
    blocks[TILES] = 1
    rel[TILES] = jnp.full_like(rel[TILES], -1)
    weights[...] = jnp.zeros_like(weights)
    lately[...] = jnp.zeros_like(lately)

    def following(t, j):
        end = j + 1 >= blocks[t]
        return jnp.minimum(t + jnp.where(end, 1, 0), TILES), jnp.where(end, 0, j + 1)

    @pl.when(safe)
    def _():
        def settle(t, u):
            acc[rows_of(t), :] += part[u]
            tot[rows_of(t), :] += part_tot[u]

        def steps(together):
            def step(_, state):
                t, j, before, at = state
                tiles = []
                for u in range(together):
                    out, out_tot = product(weights[(u + 1) % 2], at, BLOCK), lately[(u + 1) % 2]
                    if u:
                        same = before == tiles[-1]
                        out = out + jnp.where(same, part[u - 1], 0.0)
                        out_tot = out_tot + jnp.where(same, part_tot[u - 1], 0.0)
                    part[u] = out
                    part_tot[u] = out_tot
                    weigh(t, j * BLOCK, u % 2)
                    tiles.append(before)
                    before, at = t, j * BLOCK
                    t, j = following(t, j)
                for u in range(together - 1):
                    @pl.when(tiles[u] != tiles[u + 1])
                    def _():
                        settle(tiles[u], u)
                settle(tiles[-1], together - 1)
                return t, j, before, at

            return step

        zero = jnp.int32(0)
        state = (zero, zero, zero + TILES, zero)
        state = lax.fori_loop(0, count // TOGETHER, steps(TOGETHER), state)
        state = lax.fori_loop(0, (count % TOGETHER + FEW - 1) // FEW, steps(FEW), state)
        _, _, before, at = state
        part[0] = product(weights[1], at, BLOCK)
        part_tot[0] = lately[1]
        settle(before, 0)

    @pl.when(jnp.logical_not(safe))
    def _():
        @pl.loop(0, TILES)
        def _(t):
            top[...] = jnp.full_like(top, -1e30)

            @pl.loop(0, blocks[t] * (BLOCK // CHUNK))
            def _(j):
                guarded(t, j * CHUNK)

    for t in range(TILES):
        rows = slice(t * M, (t + 1) * M)
        done = acc[rows, :] / jnp.sum(tot[rows, :], axis=1, keepdims=True)
        for r in range(TILE_RUNS):
            rows = pl.ds(pl.multiple_of(run_at[t * TILE_RUNS + r] * SPAN, 8), SPAN)
            for h in range(HEADS_HERE):
                out32[rows, h * D:(h + 1) * D] = done[h * TILE_ROWS + r * SPAN:h * TILE_ROWS + (r + 1) * SPAN]

    o_ref[...] = out32[...].astype(jnp.bfloat16)


def attend(run_index, q, k, v):
    smem = pl.BlockSpec(memory_space=pltpu.SMEM)
    rows = PEERS * ROWS
    return pl.pallas_call(
        attend_kernel,
        out_shape=jax.ShapeDtypeStruct((rows, 256), jnp.bfloat16),
        in_specs=[smem] + [pl.BlockSpec(memory_space=HBM)] * 3,
        out_specs=pl.BlockSpec(memory_space=pltpu.VMEM),
        scratch_shapes=[
            pltpu.VMEM((rows, 256), jnp.bfloat16),
            pltpu.VMEM((RUNS // 2 * KROWS, D), jnp.bfloat16),
            pltpu.VMEM((SEQ, D), jnp.bfloat16),
            pltpu.VMEM((SEQ, D), jnp.bfloat16),
            pltpu.VMEM((SEQ, D), jnp.bfloat16),
            pltpu.VMEM((TILES * M + M, D), jnp.bfloat16),
            pltpu.VMEM((TILES + 1, TILE_ROWS, 128), jnp.int32),
            pltpu.VMEM((TILES * M + M, D), jnp.float32),
            pltpu.VMEM((TILES * M + M, 128), jnp.float32),
            pltpu.VMEM((M, 128), jnp.float32),
            pltpu.VMEM((2, M, BLOCK), jnp.bfloat16),
            pltpu.VMEM((2, M, 128), jnp.float32),
            pltpu.VMEM((TOGETHER, M, D), jnp.float32),
            pltpu.VMEM((TOGETHER, M, 128), jnp.float32),
            pltpu.VMEM((rows, 256), jnp.float32),
            pltpu.SMEM((RUNS,), jnp.int32),
            pltpu.SMEM((RUNS,), jnp.int32),
            pltpu.SMEM((GROUP_RUNS + 1,), jnp.int32),
            pltpu.SMEM((GROUP_RUNS + 1,), jnp.int32),
            pltpu.SMEM((TILES + 1,), jnp.int32),
            pltpu.SemaphoreType.DMA((3 * SPLIT,)),
        ],
        compiler_params=pltpu.CompilerParams(vmem_limit_bytes=56 << 20),
        name="attend",
    )(run_index, q, k, v)


def on_device(queries, keys, values, positions):
    qg, kg, vg = gather(queries, keys, values, positions.reshape(1, ROWS))
    run_index = kg.reshape(RUNS // 2, KROWS, D)[:, ROWS, :2].astype(jnp.int32).reshape(RUNS)
    o = attend(run_index, qg.reshape(PEERS * ROWS, 256),
               kg.reshape(RUNS // 2 * KROWS, D), vg.reshape(SEQ, D))
    return give_back(o.reshape(PEERS, ROWS, 256))


def solution(mesh):
    return jax.shard_map(
        on_device,
        mesh=mesh,
        in_specs=(
            P(("outer", "inner"), None),
            P(("outer", "inner"), None),
            P(("outer", "inner"), None),
            P(("outer", "inner")),
        ),
        out_specs=P(("outer", "inner"), None),
        check_vma=False,
    )
```

```python
import functools
import jax
import jax.numpy as jnp
from jax import lax
from jax.experimental import pallas as pl
from jax.experimental.pallas import tpu as pltpu
from jax.sharding import PartitionSpec as P

HEADS = 32
KV_HEADS = 4
D = 128
SPAN = 56
SEQ = 14336
RUNS = SEQ // SPAN
ROWS = 112
KROWS = 128
PEERS = 8
WIDE = 512
MESH = pl.DeviceIdType.MESH
LOG2E = 1.4426950408889634
SCALE = D ** -0.5 * LOG2E
HBM = pl.ANY
BLOCK = 512
TOGETHER = 16
FEW = 4
PREP = 8
SPLIT = 4
CHUNK = 256
TILE_RUNS = 2
GROUP_RUNS = 2 * PEERS
TILES = GROUP_RUNS // TILE_RUNS
HEADS_HERE = 4
TILE_ROWS = TILE_RUNS * SPAN
M = HEADS_HERE * TILE_ROWS
SAFE = 90.0


def coords():
    outer, inner = lax.axis_index("outer"), lax.axis_index("inner")
    y, xh, core = outer // 4, (outer // 2) % 2, outer % 2
    return xh * 2 + inner % 2, y, inner // 2, core


def at(x, y, z, core):
    return ((y * 4 + (x // 2) * 2 + core), z * 2 + x % 2)


def greet(devices):
    barrier = pltpu.get_barrier_semaphore()
    for device in devices:
        pl.semaphore_signal(barrier, inc=1, device_id=device, device_id_type=MESH)
    pl.semaphore_wait(barrier, len(devices))


def group_peers(x, y, z, core):
    return [(x, y, (z + d // 2) % 4, (core + d % 2) % 2) for d in range(1, PEERS)]


def slot_of(z, core):
    return z * 2 + core


def gather_kernel(q_ref, k_ref, v_ref, pos_ref, qg_ref, kg_ref, vg_ref,
                  q_send, q_recv, z_send, z_recv, l_sem,
                  a_send, a_recv, b_send, b_recv, s_send, s_recv, news_ref):
    x, y, z, core = coords()
    xr, xl, xo = (x + 1) % 4, (x + 3) % 4, (x + 2) % 4
    yr, yl, yo = (y + 1) % 4, (y + 3) % 4, (y + 2) % 4
    peers = group_peers(x, y, z, core)
    arrays = ((k_ref, kg_ref), (v_ref, vg_ref))
    deep = (KROWS, ROWS)
    def slot(i, rows, start=0):
        return arrays[i][1].at[core, y, x, pl.ds(pl.multiple_of(z * deep[i] + start, 16), rows), :]

    def columns(i, head):
        return arrays[i][0].at[:, pl.ds(pl.multiple_of(head * D, D), D)]

    runs = pos_ref[...].astype(jnp.float32) * (1.0 / SPAN)
    lane = lax.broadcasted_iota(jnp.int32, (1, ROWS), 1)
    later = jnp.sum(jnp.where(lane == SPAN, runs, 0.0), axis=1, keepdims=True)
    news_ref[...] = jnp.zeros_like(news_ref)
    news_ref[:, :ROWS] = jnp.broadcast_to(jnp.where(lane == 1, later, runs), (KROWS - ROWS, ROWS)).astype(jnp.bfloat16)
    me = slot_of(z, core)
    lc = []
    for i, (src, dst) in enumerate(((columns(0, z), slot(0, ROWS)), (columns(1, z), slot(1, ROWS)),
                                    (news_ref, slot(0, KROWS - ROWS, ROWS)),
                                    (q_ref.at[:, pl.ds(pl.multiple_of(me * WIDE, WIDE), WIDE)], qg_ref.at[me]))):
        c = pltpu.make_async_copy(src, dst, l_sem.at[i])
        c.start()
        lc.append(c)
    greet([at(*p) for p in peers]
          + [at(bx, y, z, core) for bx in (xl, xr)] + [at(x, by, z, core) for by in (yl, yr)])

    sent = []

    def send(src, dst, ssem, rsem, to):
        c = pltpu.make_async_remote_copy(
            src_ref=src, dst_ref=dst, send_sem=ssem, recv_sem=rsem,
            device_id=at(*to), device_id_type=MESH)
        c.start()
        sent.append(c)
        return c

    def drain(keep):
        while len(sent) > keep:
            sent.pop(0).wait_send()

    zc = []
    for d in range(1, 4):
        zz = (z + d) % 4
        for i in range(2):
            zc.append(send(columns(i, zz), slot(i, ROWS), z_send.at[i, d], z_recv.at[i, d], (x, y, zz, core)))
        zc.append(send(news_ref, slot(0, KROWS - ROWS, ROWS), z_send.at[2, d], z_recv.at[2, d], (x, y, zz, core)))
    for c in lc:
        c.wait()
    for c in zc:
        c.wait_recv()
    qc = []
    for d, p in zip(range(1, PEERS), peers):
        t = slot_of(p[2], p[3])
        qc.append(send(q_ref.at[:, pl.ds(pl.multiple_of(t * WIDE, WIDE), WIDE)],
                       qg_ref.at[me], q_send.at[d], q_recv.at[d], p))

    def block(i, bx, by, h=None):
        ref, half = arrays[i][1], 2 * deep[i]
        if h is None:
            return ref.at[core, by, bx]
        return ref.at[core, by, bx, pl.ds(h * half, half), :]

    sibling = (x, y, z, 1 - core)
    along_x = ("x", (xl, xr, xo))
    along_y = ("y", (yl, yr, yo))
    axes = ((along_x, along_y), (along_y, along_x))

    def move(axis, bx, by, n):
        if n == 0:
            return bx, by
        return (axis[1][n - 1], by) if axis[0] == "x" else (bx, axis[1][n - 1])

    def pair(axis):
        return ((xr, y), (xl, y)) if axis[0] == "x" else ((x, yr), (x, yl))

    def spread(i, axis, bx, by, ssem, rsem):
        ref = block(i, bx, by)
        return [send(ref, ref, ssem.at[k], rsem.at[k], (t[0], t[1], z, core)) for k, t in enumerate(pair(axis))]

    def relay(i, axis, bx, by, got, ssem, rsem, then):
        out = []
        for n in (1, 2):
            got[n - 1].wait_recv()
            ux, uy = move(axis, bx, by, n)
            ref, to = block(i, ux, uy, n - 1), pair(axis)[n - 1]
            out.append(send(ref, ref, ssem.at[n + 1], rsem.at[n + 1], (to[0], to[1], z, core)))
            then(n, ux, uy)
        return out

    sib = []

    def hand(i, n, bx, by):
        ref = block(i, bx, by)
        sib.append(send(ref, ref, s_send.at[i, n], s_recv.at[i, n], sibling))

    second = [[None] * 4, [None] * 4]

    def start_second(i, n):
        bx, by = move(axes[i][0], x, y, n)
        second[i][n] = spread(i, axes[i][1], bx, by, b_send.at[i, n], b_recv.at[i, n])
        hand(i, 4 * n, bx, by)

    first = [spread(i, axes[i][0], x, y, a_send.at[i], a_recv.at[i]) for i in range(2)]
    for i in range(2):
        start_second(i, 0)
    far = [relay(i, axes[i][0], x, y, first[i], a_send.at[i], a_recv.at[i],
                 lambda n, ux, uy, i=i: start_second(i, n)) for i in range(2)]
    last = [[None] * 4, [None] * 4]

    def relay_second(i, n):
        bx, by = move(axes[i][0], x, y, n)
        last[i][n] = relay(i, axes[i][1], bx, by, second[i][n], b_send.at[i, n], b_recv.at[i, n],
                           lambda m, ux, uy: hand(i, 4 * n + m, ux, uy))

    drain(24)
    for i in range(2):
        relay_second(i, 0)
    for i in range(2):
        for c in far[i]:
            c.wait_recv()
        start_second(i, 3)
    for n in range(1, 4):
        drain(24)
        for i in range(2):
            relay_second(i, n)
    for n in range(4):
        for i in range(2):
            drain(16)
            for c in last[i][n]:
                c.wait_recv()
            hand(i, 4 * n + 3, *move(axes[i][1], *move(axes[i][0], x, y, n), 3))
    for c in qc:
        c.wait_recv()
    for c in sib:
        c.wait_recv()
    drain(0)


def gather(q, k, v, positions):
    dma = pltpu.SemaphoreType.DMA
    return pl.pallas_call(
        gather_kernel,
        out_shape=(
            jax.ShapeDtypeStruct((PEERS, ROWS, WIDE), jnp.bfloat16),
            jax.ShapeDtypeStruct((2, 4, 4, 4 * KROWS, D), jnp.bfloat16),
            jax.ShapeDtypeStruct((2, 4, 4, 4 * ROWS, D), jnp.bfloat16),
        ),
        in_specs=[pl.BlockSpec(memory_space=HBM)] * 3 + [pl.BlockSpec(memory_space=pltpu.VMEM)],
        out_specs=[pl.BlockSpec(memory_space=HBM)] * 3,
        scratch_shapes=[
            dma((PEERS,)), dma((PEERS,)), dma((3, 4)), dma((3, 4)), dma((4,)),
            dma((2, 4)), dma((2, 4)), dma((2, 4, 4)), dma((2, 4, 4)), dma((2, 16)), dma((2, 16)),
            pltpu.VMEM((KROWS - ROWS, D), jnp.bfloat16),
        ],
        compiler_params=pltpu.CompilerParams(collective_id=0, has_side_effects=True),
        name="gather",
    )(q, k, v, positions)


def return_kernel(o_ref, out_ref, send_sem, recv_sem, l_sem):
    x, y, z, core = coords()
    peers = group_peers(x, y, z, core)
    me = slot_of(z, core)
    there = out_ref.at[:, pl.ds(pl.multiple_of(me * WIDE, WIDE), WIDE)]
    own = pltpu.make_async_copy(o_ref.at[me], there, l_sem)
    own.start()
    greet([at(*p) for p in peers])
    copies = []
    for d, p in zip(range(1, PEERS), peers):
        c = pltpu.make_async_remote_copy(
            src_ref=o_ref.at[slot_of(p[2], p[3])], dst_ref=there,
            send_sem=send_sem.at[d], recv_sem=recv_sem.at[d],
            device_id=at(*p), device_id_type=MESH)
        c.start()
        copies.append(c)
    own.wait()
    for c in copies:
        c.wait_recv()
    for c in copies:
        c.wait_send()


def give_back(o):
    dma = pltpu.SemaphoreType.DMA
    return pl.pallas_call(
        return_kernel,
        out_shape=jax.ShapeDtypeStruct((ROWS, HEADS * D), jnp.bfloat16),
        in_specs=[pl.BlockSpec(memory_space=HBM)],
        out_specs=pl.BlockSpec(memory_space=HBM),
        scratch_shapes=[dma((PEERS,)), dma((PEERS,)), dma],
        compiler_params=pltpu.CompilerParams(collective_id=1, has_side_effects=True),
        name="give_back",
    )(o)


def half_of(ref, loc, stride=ROWS):
    pair = ref[pl.ds(pl.multiple_of((loc // 2) * stride, 16), ROWS), :].astype(jnp.float32)
    return jnp.where(loc % 2 == 1, pair[SPAN:], pair[:SPAN])


def attend_kernel(run_index, q_hbm, k_hbm, v_hbm, o_ref,
                  q_raw, k_raw, v_raw, k_sorted, v_sorted, q_tile, rel, acc, tot, top, weights, lately, part, part_tot, out32,
                  key_at, own, run_at, run_pos, blocks, sem):
    copies = []
    for src, dst in ((q_hbm, q_raw), (k_hbm, k_raw), (v_hbm, v_raw)):
        size = src.shape[0] // SPLIT
        for i in range(SPLIT):
            rows = pl.ds(i * size, size)
            copies.append(pltpu.make_async_copy(src.at[rows, :], dst.at[rows, :], sem.at[len(copies)]))
            copies[-1].start()

    my_x, my_y, _, _ = coords()
    for p in range(RUNS):
        own[p] = -1
    for loc in range(RUNS):
        key_at[run_index[loc]] = loc
    for i in range(GROUP_RUNS):
        z, core, half = i // 4, (i // 2) % 2, i % 2
        loc = (core * 4 + my_y) * 32 + my_x * 8 + z * 2 + half
        own[run_index[loc]] = i
    n = jnp.int32(0)
    for p in range(RUNS):
        who = own[p]
        run_at[n] = who
        run_pos[n] = p
        n = n + jnp.where(who >= 0, 1, 0)
    for c in copies:
        c.wait()

    @pl.loop(0, RUNS // 2 // PREP)
    def _(step):
        for i in range(PREP):
            j = step * PREP + i
            rows = pl.ds(pl.multiple_of(j * ROWS, 16), ROWS)
            a, b = key_at[2 * j], key_at[2 * j + 1]
            k2 = jnp.concatenate([half_of(k_raw, a, KROWS), half_of(k_raw, b, KROWS)], axis=0).astype(jnp.bfloat16)
            k_sorted[rows, :] = k2
            v2 = jnp.concatenate([half_of(v_raw, a), half_of(v_raw, b)], axis=0).astype(jnp.bfloat16)
            v_sorted[rows, :] = v2

    ones = jnp.ones((D, D), jnp.bfloat16)
    longest = None
    for i in range(SEQ // 2048):
        keys = k_sorted[i * 2048:(i + 1) * 2048, :]
        square = jnp.dot(keys * keys, ones, preferred_element_type=jnp.float32)
        square = jnp.max(square, axis=0, keepdims=True)
        longest = square if longest is None else jnp.maximum(longest, square)
    key_norm = jnp.max(longest) * 1.01

    longest = None
    for t in range(TILES):
        scaled = [half_of(q_raw, run_at[t * TILE_RUNS + r]) for r in range(TILE_RUNS)]
        whole = jnp.concatenate(scaled, axis=0).astype(jnp.bfloat16)
        for h in range(HEADS_HERE):
            x = whole[:, h * D:(h + 1) * D]
            q_tile[t * M + h * TILE_ROWS:t * M + (h + 1) * TILE_ROWS, :] = x
            square = jnp.dot(x * x, ones, preferred_element_type=jnp.float32)
            square = jnp.max(square, axis=0, keepdims=True)
            longest = square if longest is None else jnp.maximum(longest, square)
    query_norm = jnp.max(longest) * 1.01
    safe = query_norm * key_norm * (SCALE * SCALE) < SAFE * SAFE
    acc[...] = jnp.zeros_like(acc)
    tot[...] = jnp.zeros_like(tot)

    def rows_of(t):
        return pl.ds(pl.multiple_of(t * M, M), M)

    def scores(at, off, width):
        return lax.dot_general(q_tile[at, :], k_sorted[pl.ds(pl.multiple_of(off, 128), width), :],
                               (((1,), (1,)), ((), ())), preferred_element_type=jnp.float32) * SCALE

    def product(p, off, width):
        return jnp.dot(p, v_sorted[pl.ds(pl.multiple_of(off, 128), width), :],
                       preferred_element_type=jnp.float32)

    def seen(t, off):
        see = rel[t] >= off
        return jnp.concatenate([see] * HEADS_HERE, axis=0)

    def weigh(t, off, slot):
        at, total = rows_of(t), None
        for i in range(BLOCK // CHUNK):
            s = scores(at, off + i * CHUNK, CHUNK)
            for w in range(0, CHUNK, 128):
                p = jnp.where(seen(t, off + i * CHUNK + w), jnp.exp2(s[:, w:w + 128]), 0.0)
                total = p if total is None else total + p
                weights[slot, :, i * CHUNK + w:i * CHUNK + w + 128] = p.astype(jnp.bfloat16)
        lately[slot] = total

    def guarded(t, off):
        at = rows_of(t)
        s = scores(at, off, CHUNK)
        cols, vis, best = [], [], top[...]
        for w in range(CHUNK // 128):
            see = seen(t, off + w * 128)
            col = jnp.where(see, s[:, w * 128:(w + 1) * 128], -1e30)
            cols.append(col)
            vis.append(see)
            best = jnp.maximum(best, jnp.max(col, axis=1, keepdims=True))
        fade = jnp.exp2(top[...] - best)
        top[...] = best
        total = tot[at, :] * fade
        parts = []
        for col, see in zip(cols, vis):
            p = jnp.where(see, jnp.exp2(col - best), 0.0)
            total = total + p
            parts.append(p.astype(jnp.bfloat16))
        tot[at, :] = total
        acc[at, :] = acc[at, :] * fade + product(jnp.concatenate(parts, axis=1), off, CHUNK)

    count = jnp.int32(0)
    for t in range(TILES):
        for r in range(TILE_RUNS):
            first = run_pos[t * TILE_RUNS + r] * SPAN
            rel[t, r * SPAN:(r + 1) * SPAN, :] = (lax.broadcasted_iota(jnp.int32, (SPAN, 128), 0)
                                                  - lax.broadcasted_iota(jnp.int32, (SPAN, 128), 1) + first)
        high = run_pos[t * TILE_RUNS + TILE_RUNS - 1] * SPAN + SPAN
        blocks[t] = (high + BLOCK - 1) // BLOCK
        count = count + blocks[t]
    blocks[TILES] = 1
    rel[TILES] = jnp.full_like(rel[TILES], -1)
    weights[...] = jnp.zeros_like(weights)
    lately[...] = jnp.zeros_like(lately)

    def following(t, j):
        end = j + 1 >= blocks[t]
        return jnp.minimum(t + jnp.where(end, 1, 0), TILES), jnp.where(end, 0, j + 1)

    @pl.when(safe)
    def _():
        def settle(t, u):
            acc[rows_of(t), :] += part[u]
            tot[rows_of(t), :] += part_tot[u]

        def steps(together):
            def step(_, state):
                t, j, before, at = state
                tiles = []
                for u in range(together):
                    out, out_tot = product(weights[(u + 1) % 2], at, BLOCK), lately[(u + 1) % 2]
                    if u:
                        same = before == tiles[-1]
                        out = out + jnp.where(same, part[u - 1], 0.0)
                        out_tot = out_tot + jnp.where(same, part_tot[u - 1], 0.0)
                    part[u] = out
                    part_tot[u] = out_tot
                    weigh(t, j * BLOCK, u % 2)
                    tiles.append(before)
                    before, at = t, j * BLOCK
                    t, j = following(t, j)
                for u in range(together - 1):
                    @pl.when(tiles[u] != tiles[u + 1])
                    def _():
                        settle(tiles[u], u)
                settle(tiles[-1], together - 1)
                return t, j, before, at

            return step

        zero = jnp.int32(0)
        state = (zero, zero, zero + TILES, zero)
        state = lax.fori_loop(0, count // TOGETHER, steps(TOGETHER), state)
        state = lax.fori_loop(0, (count % TOGETHER + FEW - 1) // FEW, steps(FEW), state)
        _, _, before, at = state
        part[0] = product(weights[1], at, BLOCK)
        part_tot[0] = lately[1]
        settle(before, 0)

    @pl.when(jnp.logical_not(safe))
    def _():
        @pl.loop(0, TILES)
        def _(t):
            top[...] = jnp.full_like(top, -1e30)

            @pl.loop(0, blocks[t] * (BLOCK // CHUNK))
            def _(j):
                guarded(t, j * CHUNK)

    for t in range(TILES):
        rows = slice(t * M, (t + 1) * M)
        done = acc[rows, :] / jnp.sum(tot[rows, :], axis=1, keepdims=True)
        for r in range(TILE_RUNS):
            rows = pl.ds(pl.multiple_of(run_at[t * TILE_RUNS + r] * SPAN, 8), SPAN)
            for h in range(HEADS_HERE):
                out32[rows, h * D:(h + 1) * D] = done[h * TILE_ROWS + r * SPAN:h * TILE_ROWS + (r + 1) * SPAN]

    o_ref[...] = out32[...].astype(jnp.bfloat16)


def attend(run_index, q, k, v):
    smem = pl.BlockSpec(memory_space=pltpu.SMEM)
    rows = PEERS * ROWS
    return pl.pallas_call(
        attend_kernel,
        out_shape=jax.ShapeDtypeStruct((rows, WIDE), jnp.bfloat16),
        in_specs=[smem] + [pl.BlockSpec(memory_space=HBM)] * 3,
        out_specs=pl.BlockSpec(memory_space=pltpu.VMEM),
        scratch_shapes=[
            pltpu.VMEM((rows, WIDE), jnp.bfloat16),
            pltpu.VMEM((RUNS // 2 * KROWS, D), jnp.bfloat16),
            pltpu.VMEM((SEQ, D), jnp.bfloat16),
            pltpu.VMEM((SEQ, D), jnp.bfloat16),
            pltpu.VMEM((SEQ, D), jnp.bfloat16),
            pltpu.VMEM((TILES * M + M, D), jnp.bfloat16),
            pltpu.VMEM((TILES + 1, TILE_ROWS, 128), jnp.int32),
            pltpu.VMEM((TILES * M + M, D), jnp.float32),
            pltpu.VMEM((TILES * M + M, 128), jnp.float32),
            pltpu.VMEM((M, 128), jnp.float32),
            pltpu.VMEM((2, M, BLOCK), jnp.bfloat16),
            pltpu.VMEM((2, M, 128), jnp.float32),
            pltpu.VMEM((TOGETHER, M, D), jnp.float32),
            pltpu.VMEM((TOGETHER, M, 128), jnp.float32),
            pltpu.VMEM((rows, WIDE), jnp.float32),
            pltpu.SMEM((RUNS,), jnp.int32),
            pltpu.SMEM((RUNS,), jnp.int32),
            pltpu.SMEM((GROUP_RUNS + 1,), jnp.int32),
            pltpu.SMEM((GROUP_RUNS + 1,), jnp.int32),
            pltpu.SMEM((TILES + 1,), jnp.int32),
            pltpu.SemaphoreType.DMA((3 * SPLIT,)),
        ],
        compiler_params=pltpu.CompilerParams(vmem_limit_bytes=56 << 20),
        name="attend",
    )(run_index, q, k, v)


def on_device(queries, keys, values, positions):
    qg, kg, vg = gather(queries, keys, values, positions.reshape(1, ROWS))
    run_index = kg.reshape(RUNS // 2, KROWS, D)[:, ROWS, :2].astype(jnp.int32).reshape(RUNS)
    o = attend(run_index, qg.reshape(PEERS * ROWS, WIDE),
               kg.reshape(RUNS // 2 * KROWS, D), vg.reshape(SEQ, D))
    return give_back(o.reshape(PEERS, ROWS, WIDE))


def solution(mesh):
    return jax.shard_map(
        on_device,
        mesh=mesh,
        in_specs=(
            P(("outer", "inner"), None),
            P(("outer", "inner"), None),
            P(("outer", "inner"), None),
            P(("outer", "inner")),
        ),
        out_specs=P(("outer", "inner"), None),
        check_vma=False,
    )
```

```python
import functools
import jax
import jax.numpy as jnp
from jax import lax
from jax.experimental import pallas as pl
from jax.experimental.pallas import tpu as pltpu
from jax.sharding import PartitionSpec as P

HEADS = 32
KV_HEADS = 4
D = 128
SPAN = 56
SEQ = 14336
RUNS = SEQ // SPAN
ROWS = 112
KROWS = 128
PEERS = 8
FARTHEST_FIRST = (4, 5, 2, 6, 3, 7, 1)
WIDE = 512
MESH = pl.DeviceIdType.MESH
LOG2E = 1.4426950408889634
SCALE = D ** -0.5 * LOG2E
HBM = pl.ANY
BLOCK = 512
TOGETHER = 16
FEW = 4
PREP = 8
SPLIT = 4
CHUNK = 256
TILE_RUNS = 2
GROUP_RUNS = 2 * PEERS
TILES = GROUP_RUNS // TILE_RUNS
HEADS_HERE = 4
TILE_ROWS = TILE_RUNS * SPAN
M = HEADS_HERE * TILE_ROWS
SAFE = 90.0


def coords():
    outer, inner = lax.axis_index("outer"), lax.axis_index("inner")
    y, xh, core = outer // 4, (outer // 2) % 2, outer % 2
    return xh * 2 + inner % 2, y, inner // 2, core


def at(x, y, z, core):
    return ((y * 4 + (x // 2) * 2 + core), z * 2 + x % 2)


def greet(devices):
    barrier = pltpu.get_barrier_semaphore()
    for device in devices:
        pl.semaphore_signal(barrier, inc=1, device_id=device, device_id_type=MESH)
    pl.semaphore_wait(barrier, len(devices))


def group_peers(x, y, z, core):
    return [(x, y, (z + d // 2) % 4, (core + d % 2) % 2) for d in FARTHEST_FIRST]


def slot_of(z, core):
    return z * 2 + core


def gather_kernel(q_ref, k_ref, v_ref, pos_ref, qg_ref, kg_ref, vg_ref,
                  q_send, q_recv, z_send, z_recv, l_sem,
                  a_send, a_recv, b_send, b_recv, s_send, s_recv, news_ref):
    x, y, z, core = coords()
    xr, xl, xo = (x + 1) % 4, (x + 3) % 4, (x + 2) % 4
    yr, yl, yo = (y + 1) % 4, (y + 3) % 4, (y + 2) % 4
    peers = group_peers(x, y, z, core)
    arrays = ((k_ref, kg_ref), (v_ref, vg_ref))
    deep = (KROWS, ROWS)
    def slot(i, rows, start=0):
        return arrays[i][1].at[core, y, x, pl.ds(pl.multiple_of(z * deep[i] + start, 16), rows), :]

    def columns(i, head):
        return arrays[i][0].at[:, pl.ds(pl.multiple_of(head * D, D), D)]

    runs = pos_ref[...].astype(jnp.float32) * (1.0 / SPAN)
    lane = lax.broadcasted_iota(jnp.int32, (1, ROWS), 1)
    later = jnp.sum(jnp.where(lane == SPAN, runs, 0.0), axis=1, keepdims=True)
    news_ref[...] = jnp.zeros_like(news_ref)
    news_ref[:, :ROWS] = jnp.broadcast_to(jnp.where(lane == 1, later, runs), (KROWS - ROWS, ROWS)).astype(jnp.bfloat16)
    me = slot_of(z, core)
    lc = []
    for i, (src, dst) in enumerate(((columns(0, z), slot(0, ROWS)), (columns(1, z), slot(1, ROWS)),
                                    (news_ref, slot(0, KROWS - ROWS, ROWS)),
                                    (q_ref.at[:, pl.ds(pl.multiple_of(me * WIDE, WIDE), WIDE)], qg_ref.at[me]))):
        c = pltpu.make_async_copy(src, dst, l_sem.at[i])
        c.start()
        lc.append(c)
    greet([at(*p) for p in peers]
          + [at(bx, y, z, core) for bx in (xl, xr)] + [at(x, by, z, core) for by in (yl, yr)])

    sent = []

    def send(src, dst, ssem, rsem, to):
        c = pltpu.make_async_remote_copy(
            src_ref=src, dst_ref=dst, send_sem=ssem, recv_sem=rsem,
            device_id=at(*to), device_id_type=MESH)
        c.start()
        sent.append(c)
        return c

    def drain(keep):
        while len(sent) > keep:
            sent.pop(0).wait_send()

    zc = []
    for d in range(1, 4):
        zz = (z + d) % 4
        for i in range(2):
            zc.append(send(columns(i, zz), slot(i, ROWS), z_send.at[i, d], z_recv.at[i, d], (x, y, zz, core)))
        zc.append(send(news_ref, slot(0, KROWS - ROWS, ROWS), z_send.at[2, d], z_recv.at[2, d], (x, y, zz, core)))
    for c in lc:
        c.wait()
    for c in zc:
        c.wait_recv()

    def block(i, bx, by, h=None):
        ref, half = arrays[i][1], 2 * deep[i]
        if h is None:
            return ref.at[core, by, bx]
        return ref.at[core, by, bx, pl.ds(h * half, half), :]

    sibling = (x, y, z, 1 - core)
    along_x = ("x", (xl, xr, xo))
    along_y = ("y", (yl, yr, yo))
    axes = ((along_x, along_y), (along_y, along_x))

    def move(axis, bx, by, n):
        if n == 0:
            return bx, by
        return (axis[1][n - 1], by) if axis[0] == "x" else (bx, axis[1][n - 1])

    def pair(axis):
        return ((xr, y), (xl, y)) if axis[0] == "x" else ((x, yr), (x, yl))

    def spread(i, axis, bx, by, ssem, rsem):
        ref = block(i, bx, by)
        return [send(ref, ref, ssem.at[k], rsem.at[k], (t[0], t[1], z, core)) for k, t in enumerate(pair(axis))]

    def relay(i, axis, bx, by, got, ssem, rsem, then):
        out = []
        for n in (1, 2):
            got[n - 1].wait_recv()
            ux, uy = move(axis, bx, by, n)
            ref, to = block(i, ux, uy, n - 1), pair(axis)[n - 1]
            out.append(send(ref, ref, ssem.at[n + 1], rsem.at[n + 1], (to[0], to[1], z, core)))
            then(n, ux, uy)
        return out

    sib = []

    def hand(i, n, bx, by):
        ref = block(i, bx, by)
        sib.append(send(ref, ref, s_send.at[i, n], s_recv.at[i, n], sibling))

    second = [[None] * 4, [None] * 4]

    def start_second(i, n):
        bx, by = move(axes[i][0], x, y, n)
        second[i][n] = spread(i, axes[i][1], bx, by, b_send.at[i, n], b_recv.at[i, n])
        hand(i, 4 * n, bx, by)

    first = [spread(i, axes[i][0], x, y, a_send.at[i], a_recv.at[i]) for i in range(2)]
    for i in range(2):
        start_second(i, 0)
    qc = []
    for d, p in zip(FARTHEST_FIRST, peers):
        t = slot_of(p[2], p[3])
        qc.append(send(q_ref.at[:, pl.ds(pl.multiple_of(t * WIDE, WIDE), WIDE)],
                       qg_ref.at[me], q_send.at[d], q_recv.at[d], p))
    far = [relay(i, axes[i][0], x, y, first[i], a_send.at[i], a_recv.at[i],
                 lambda n, ux, uy, i=i: start_second(i, n)) for i in range(2)]
    last = [[None] * 4, [None] * 4]

    def relay_second(i, n):
        bx, by = move(axes[i][0], x, y, n)
        last[i][n] = relay(i, axes[i][1], bx, by, second[i][n], b_send.at[i, n], b_recv.at[i, n],
                           lambda m, ux, uy: hand(i, 4 * n + m, ux, uy))

    drain(24)
    for i in range(2):
        relay_second(i, 0)
    for i in range(2):
        for c in far[i]:
            c.wait_recv()
        start_second(i, 3)
    for n in range(1, 4):
        drain(24)
        for i in range(2):
            relay_second(i, n)
    for n in range(4):
        for i in range(2):
            drain(16)
            for c in last[i][n]:
                c.wait_recv()
            hand(i, 4 * n + 3, *move(axes[i][1], *move(axes[i][0], x, y, n), 3))
    for c in qc:
        c.wait_recv()
    for c in sib:
        c.wait_recv()
    drain(0)


def gather(q, k, v, positions):
    dma = pltpu.SemaphoreType.DMA
    return pl.pallas_call(
        gather_kernel,
        out_shape=(
            jax.ShapeDtypeStruct((PEERS, ROWS, WIDE), jnp.bfloat16),
            jax.ShapeDtypeStruct((2, 4, 4, 4 * KROWS, D), jnp.bfloat16),
            jax.ShapeDtypeStruct((2, 4, 4, 4 * ROWS, D), jnp.bfloat16),
        ),
        in_specs=[pl.BlockSpec(memory_space=HBM)] * 3 + [pl.BlockSpec(memory_space=pltpu.VMEM)],
        out_specs=[pl.BlockSpec(memory_space=HBM)] * 3,
        scratch_shapes=[
            dma((PEERS,)), dma((PEERS,)), dma((3, 4)), dma((3, 4)), dma((4,)),
            dma((2, 4)), dma((2, 4)), dma((2, 4, 4)), dma((2, 4, 4)), dma((2, 16)), dma((2, 16)),
            pltpu.VMEM((KROWS - ROWS, D), jnp.bfloat16),
        ],
        compiler_params=pltpu.CompilerParams(collective_id=0, has_side_effects=True),
        name="gather",
    )(q, k, v, positions)


def return_kernel(o_ref, out_ref, send_sem, recv_sem, l_sem):
    x, y, z, core = coords()
    peers = group_peers(x, y, z, core)
    me = slot_of(z, core)
    there = out_ref.at[:, pl.ds(pl.multiple_of(me * WIDE, WIDE), WIDE)]
    own = pltpu.make_async_copy(o_ref.at[me], there, l_sem)
    own.start()
    greet([at(*p) for p in peers])
    copies = []
    for d, p in zip(FARTHEST_FIRST, peers):
        c = pltpu.make_async_remote_copy(
            src_ref=o_ref.at[slot_of(p[2], p[3])], dst_ref=there,
            send_sem=send_sem.at[d], recv_sem=recv_sem.at[d],
            device_id=at(*p), device_id_type=MESH)
        c.start()
        copies.append(c)
    own.wait()
    for c in copies:
        c.wait_recv()
    for c in copies:
        c.wait_send()


def give_back(o):
    dma = pltpu.SemaphoreType.DMA
    return pl.pallas_call(
        return_kernel,
        out_shape=jax.ShapeDtypeStruct((ROWS, HEADS * D), jnp.bfloat16),
        in_specs=[pl.BlockSpec(memory_space=HBM)],
        out_specs=pl.BlockSpec(memory_space=HBM),
        scratch_shapes=[dma((PEERS,)), dma((PEERS,)), dma],
        compiler_params=pltpu.CompilerParams(collective_id=1, has_side_effects=True),
        name="give_back",
    )(o)


def half_of(ref, loc, stride=ROWS):
    pair = ref[pl.ds(pl.multiple_of((loc // 2) * stride, 16), ROWS), :].astype(jnp.float32)
    return jnp.where(loc % 2 == 1, pair[SPAN:], pair[:SPAN])


def attend_kernel(run_index, q_hbm, k_hbm, v_hbm, o_ref,
                  q_raw, k_raw, v_raw, k_sorted, v_sorted, q_tile, rel, acc, tot, top, weights, lately, part, part_tot, out32,
                  key_at, own, run_at, run_pos, blocks, sem):
    copies = []
    for src, dst in ((q_hbm, q_raw), (k_hbm, k_raw), (v_hbm, v_raw)):
        size = src.shape[0] // SPLIT
        for i in range(SPLIT):
            rows = pl.ds(i * size, size)
            copies.append(pltpu.make_async_copy(src.at[rows, :], dst.at[rows, :], sem.at[len(copies)]))
            copies[-1].start()

    my_x, my_y, _, _ = coords()
    for p in range(RUNS):
        own[p] = -1
    for loc in range(RUNS):
        key_at[run_index[loc]] = loc
    for i in range(GROUP_RUNS):
        z, core, half = i // 4, (i // 2) % 2, i % 2
        loc = (core * 4 + my_y) * 32 + my_x * 8 + z * 2 + half
        own[run_index[loc]] = i
    n = jnp.int32(0)
    for p in range(RUNS):
        who = own[p]
        run_at[n] = who
        run_pos[n] = p
        n = n + jnp.where(who >= 0, 1, 0)
    for c in copies:
        c.wait()

    @pl.loop(0, RUNS // 2 // PREP)
    def _(step):
        for i in range(PREP):
            j = step * PREP + i
            rows = pl.ds(pl.multiple_of(j * ROWS, 16), ROWS)
            a, b = key_at[2 * j], key_at[2 * j + 1]
            k2 = jnp.concatenate([half_of(k_raw, a, KROWS), half_of(k_raw, b, KROWS)], axis=0).astype(jnp.bfloat16)
            k_sorted[rows, :] = k2
            v2 = jnp.concatenate([half_of(v_raw, a), half_of(v_raw, b)], axis=0).astype(jnp.bfloat16)
            v_sorted[rows, :] = v2

    ones = jnp.ones((D, D), jnp.bfloat16)
    longest = None
    for i in range(SEQ // 2048):
        keys = k_sorted[i * 2048:(i + 1) * 2048, :]
        square = jnp.dot(keys * keys, ones, preferred_element_type=jnp.float32)
        square = jnp.max(square, axis=0, keepdims=True)
        longest = square if longest is None else jnp.maximum(longest, square)
    key_norm = jnp.max(longest) * 1.01

    longest = None
    for t in range(TILES):
        scaled = [half_of(q_raw, run_at[t * TILE_RUNS + r]) for r in range(TILE_RUNS)]
        whole = jnp.concatenate(scaled, axis=0).astype(jnp.bfloat16)
        for h in range(HEADS_HERE):
            x = whole[:, h * D:(h + 1) * D]
            q_tile[t * M + h * TILE_ROWS:t * M + (h + 1) * TILE_ROWS, :] = x
            square = jnp.dot(x * x, ones, preferred_element_type=jnp.float32)
            square = jnp.max(square, axis=0, keepdims=True)
            longest = square if longest is None else jnp.maximum(longest, square)
    query_norm = jnp.max(longest) * 1.01
    safe = query_norm * key_norm * (SCALE * SCALE) < SAFE * SAFE
    acc[...] = jnp.zeros_like(acc)
    tot[...] = jnp.zeros_like(tot)

    def rows_of(t):
        return pl.ds(pl.multiple_of(t * M, M), M)

    def scores(at, off, width):
        return lax.dot_general(q_tile[at, :], k_sorted[pl.ds(pl.multiple_of(off, 128), width), :],
                               (((1,), (1,)), ((), ())), preferred_element_type=jnp.float32) * SCALE

    def product(p, off, width):
        return jnp.dot(p, v_sorted[pl.ds(pl.multiple_of(off, 128), width), :],
                       preferred_element_type=jnp.float32)

    def seen(t, off):
        see = rel[t] >= off
        return jnp.concatenate([see] * HEADS_HERE, axis=0)

    def weigh(t, off, slot):
        at, total = rows_of(t), None
        for i in range(BLOCK // CHUNK):
            s = scores(at, off + i * CHUNK, CHUNK)
            for w in range(0, CHUNK, 128):
                p = jnp.where(seen(t, off + i * CHUNK + w), jnp.exp2(s[:, w:w + 128]), 0.0)
                total = p if total is None else total + p
                weights[slot, :, i * CHUNK + w:i * CHUNK + w + 128] = p.astype(jnp.bfloat16)
        lately[slot] = total

    def guarded(t, off):
        at = rows_of(t)
        s = scores(at, off, CHUNK)
        cols, vis, best = [], [], top[...]
        for w in range(CHUNK // 128):
            see = seen(t, off + w * 128)
            col = jnp.where(see, s[:, w * 128:(w + 1) * 128], -1e30)
            cols.append(col)
            vis.append(see)
            best = jnp.maximum(best, jnp.max(col, axis=1, keepdims=True))
        fade = jnp.exp2(top[...] - best)
        top[...] = best
        total = tot[at, :] * fade
        parts = []
        for col, see in zip(cols, vis):
            p = jnp.where(see, jnp.exp2(col - best), 0.0)
            total = total + p
            parts.append(p.astype(jnp.bfloat16))
        tot[at, :] = total
        acc[at, :] = acc[at, :] * fade + product(jnp.concatenate(parts, axis=1), off, CHUNK)

    count = jnp.int32(0)
    for t in range(TILES):
        for r in range(TILE_RUNS):
            first = run_pos[t * TILE_RUNS + r] * SPAN
            rel[t, r * SPAN:(r + 1) * SPAN, :] = (lax.broadcasted_iota(jnp.int32, (SPAN, 128), 0)
                                                  - lax.broadcasted_iota(jnp.int32, (SPAN, 128), 1) + first)
        high = run_pos[t * TILE_RUNS + TILE_RUNS - 1] * SPAN + SPAN
        blocks[t] = (high + BLOCK - 1) // BLOCK
        count = count + blocks[t]
    blocks[TILES] = 1
    rel[TILES] = jnp.full_like(rel[TILES], -1)
    weights[...] = jnp.zeros_like(weights)
    lately[...] = jnp.zeros_like(lately)

    def following(t, j):
        end = j + 1 >= blocks[t]
        return jnp.minimum(t + jnp.where(end, 1, 0), TILES), jnp.where(end, 0, j + 1)

    @pl.when(safe)
    def _():
        def settle(t, u):
            acc[rows_of(t), :] += part[u]
            tot[rows_of(t), :] += part_tot[u]

        def steps(together):
            def step(_, state):
                t, j, before, at = state
                tiles = []
                for u in range(together):
                    out, out_tot = product(weights[(u + 1) % 2], at, BLOCK), lately[(u + 1) % 2]
                    if u:
                        same = before == tiles[-1]
                        out = out + jnp.where(same, part[u - 1], 0.0)
                        out_tot = out_tot + jnp.where(same, part_tot[u - 1], 0.0)
                    part[u] = out
                    part_tot[u] = out_tot
                    weigh(t, j * BLOCK, u % 2)
                    tiles.append(before)
                    before, at = t, j * BLOCK
                    t, j = following(t, j)
                for u in range(together - 1):
                    @pl.when(tiles[u] != tiles[u + 1])
                    def _():
                        settle(tiles[u], u)
                settle(tiles[-1], together - 1)
                return t, j, before, at

            return step

        zero = jnp.int32(0)
        state = (zero, zero, zero + TILES, zero)
        state = lax.fori_loop(0, count // TOGETHER, steps(TOGETHER), state)
        state = lax.fori_loop(0, (count % TOGETHER + FEW - 1) // FEW, steps(FEW), state)
        _, _, before, at = state
        part[0] = product(weights[1], at, BLOCK)
        part_tot[0] = lately[1]
        settle(before, 0)

    @pl.when(jnp.logical_not(safe))
    def _():
        @pl.loop(0, TILES)
        def _(t):
            top[...] = jnp.full_like(top, -1e30)

            @pl.loop(0, blocks[t] * (BLOCK // CHUNK))
            def _(j):
                guarded(t, j * CHUNK)

    for t in range(TILES):
        rows = slice(t * M, (t + 1) * M)
        done = acc[rows, :] / jnp.sum(tot[rows, :], axis=1, keepdims=True)
        for r in range(TILE_RUNS):
            rows = pl.ds(pl.multiple_of(run_at[t * TILE_RUNS + r] * SPAN, 8), SPAN)
            for h in range(HEADS_HERE):
                out32[rows, h * D:(h + 1) * D] = done[h * TILE_ROWS + r * SPAN:h * TILE_ROWS + (r + 1) * SPAN]

    o_ref[...] = out32[...].astype(jnp.bfloat16)


def attend(run_index, q, k, v):
    smem = pl.BlockSpec(memory_space=pltpu.SMEM)
    rows = PEERS * ROWS
    return pl.pallas_call(
        attend_kernel,
        out_shape=jax.ShapeDtypeStruct((rows, WIDE), jnp.bfloat16),
        in_specs=[smem] + [pl.BlockSpec(memory_space=HBM)] * 3,
        out_specs=pl.BlockSpec(memory_space=pltpu.VMEM),
        scratch_shapes=[
            pltpu.VMEM((rows, WIDE), jnp.bfloat16),
            pltpu.VMEM((RUNS // 2 * KROWS, D), jnp.bfloat16),
            pltpu.VMEM((SEQ, D), jnp.bfloat16),
            pltpu.VMEM((SEQ, D), jnp.bfloat16),
            pltpu.VMEM((SEQ, D), jnp.bfloat16),
            pltpu.VMEM((TILES * M + M, D), jnp.bfloat16),
            pltpu.VMEM((TILES + 1, TILE_ROWS, 128), jnp.int32),
            pltpu.VMEM((TILES * M + M, D), jnp.float32),
            pltpu.VMEM((TILES * M + M, 128), jnp.float32),
            pltpu.VMEM((M, 128), jnp.float32),
            pltpu.VMEM((2, M, BLOCK), jnp.bfloat16),
            pltpu.VMEM((2, M, 128), jnp.float32),
            pltpu.VMEM((TOGETHER, M, D), jnp.float32),
            pltpu.VMEM((TOGETHER, M, 128), jnp.float32),
            pltpu.VMEM((rows, WIDE), jnp.float32),
            pltpu.SMEM((RUNS,), jnp.int32),
            pltpu.SMEM((RUNS,), jnp.int32),
            pltpu.SMEM((GROUP_RUNS + 1,), jnp.int32),
            pltpu.SMEM((GROUP_RUNS + 1,), jnp.int32),
            pltpu.SMEM((TILES + 1,), jnp.int32),
            pltpu.SemaphoreType.DMA((3 * SPLIT,)),
        ],
        compiler_params=pltpu.CompilerParams(vmem_limit_bytes=56 << 20),
        name="attend",
    )(run_index, q, k, v)


def on_device(queries, keys, values, positions):
    qg, kg, vg = gather(queries, keys, values, positions.reshape(1, ROWS))
    run_index = kg.reshape(RUNS // 2, KROWS, D)[:, ROWS, :2].astype(jnp.int32).reshape(RUNS)
    o = attend(run_index, qg.reshape(PEERS * ROWS, WIDE),
               kg.reshape(RUNS // 2 * KROWS, D), vg.reshape(SEQ, D))
    return give_back(o.reshape(PEERS, ROWS, WIDE))


def solution(mesh):
    return jax.shard_map(
        on_device,
        mesh=mesh,
        in_specs=(
            P(("outer", "inner"), None),
            P(("outer", "inner"), None),
            P(("outer", "inner"), None),
            P(("outer", "inner")),
        ),
        out_specs=P(("outer", "inner"), None),
        check_vma=False,
    )
```
